128 devices in a mesh: section: 2 (over core), group: 8 (over x, z_lo), replica: 8 (over z_hi, y).
Axes of the slice: x: 4, y: 4, z: 4 (z_hi: 2, z_lo: 2; z = z_hi * 2 + z_lo), core: 2. Of those that a mesh axis runs over, the one named last changes fastest.
Arguments:
- tokens: bfloat16 [16, 1024, 768], P('replica', 'group'), may hold values from -6 to 6
- cotangent: float32 [16, 1024, 768], P('replica', 'group'), may hold values from -6 to 6
- lengths: int32 [16, 3], P('replica'), may hold values from 1 to 1022, as said below
- ln1_gain: bfloat16 [2, 768], P('section', 'group'), may hold values from 0.5 to 1.5
- ln1_bias: bfloat16 [2, 768], P('section', 'group'), may hold values from -3 to 3
- w_qkv: bfloat16 [2, 768, 2304], P('section', 'group'), may hold values from -0.21875 to 0.21875
- b_query: bfloat16 [2, 768], P('section', 'group'), may hold values from -3 to 3
- b_value: bfloat16 [2, 768], P('section', 'group'), may hold values from -3 to 3
- w_out: bfloat16 [2, 768, 768], P('section', 'group'), may hold values from -0.875 to 0.875
- b_out: bfloat16 [2, 768], P('section', 'group'), may hold values from -3 to 3
- ln2_gain: bfloat16 [2, 768], P('section', 'group'), may hold values from 0.5 to 1.5
- ln2_bias: bfloat16 [2, 768], P('section', 'group'), may hold values from -3 to 3
- w_fc: bfloat16 [2, 768, 3072], P('section', 'group'), may hold values from -0.21875 to 0.21875
- b_fc: bfloat16 [2, 3072], P('section', 'group'), may hold values from -3 to 3
- w_proj: bfloat16 [2, 3072, 768], P('section', 'group'), may hold values from -0.109375 to 0.109375
- b_proj: bfloat16 [2, 768], P('section', 'group'), may hold values from -3 to 3
Outputs:
- acts: bfloat16 [2, 16, 1024, 768], P('section', 'replica', 'group')
- in_grads: bfloat16 [2, 16, 1024, 768], P('section', 'replica', 'group')
- grad_ln1_gain: float32 [2, 768], P('section', 'group')
- grad_ln1_bias: float32 [2, 768], P('section', 'group')
- grad_w_qkv: float32 [2, 768, 2304], P('section', 'group')
- grad_b_query: float32 [2, 768], P('section', 'group')
- grad_b_value: float32 [2, 768], P('section', 'group')
- grad_w_out: float32 [2, 768, 768], P('section', 'group')
- grad_b_out: float32 [2, 768], P('section', 'group')
- grad_ln2_gain: float32 [2, 768], P('section', 'group')
- grad_ln2_bias: float32 [2, 768], P('section', 'group')
- grad_w_fc: float32 [2, 768, 3072], P('section', 'group')
- grad_b_fc: float32 [2, 3072], P('section', 'group')
- grad_w_proj: float32 [2, 3072, 768], P('section', 'group')
- grad_b_proj: float32 [2, 768], P('section', 'group')
The draws below stay inside these ranges and needn't reach their ends.
Inputs may be any that keep to these rules, and one draw needn't show every extreme that they name: In each row the three lengths sum to 1024; the first and the last lie between 1 and 127, so the middle document reaches from the first index of group to the last.
All inputs are finite; a program needn't handle non-finite values.
Results may differ from the reference program's by a relative error of at most 0.02.
Values may be sent and summed in bfloat16 or wider, within the bound.
No kernel may reach another device: no remote copies, remote signals or barrier semaphores. Data moves between devices by JAX's collectives and lax.ppermute only.
A program may use at most 256 MiB of HBM per device.

```python
import jax
import jax.numpy as jnp
from jax import lax

D = 768
HEADS = 12
HEAD = 64
FF = 3072
TOK_DEV = 128
BATCH = 16
MBTOK = 1024


def draw_lengths(key, part):
    key = jax.random.fold_in(key, 7)
    head_key, tail_key = jax.random.split(key)
    head_len = jax.random.randint(head_key, (BATCH,), 1, TOK_DEV)
    tail_len = jax.random.randint(tail_key, (BATCH,), 1, TOK_DEV)
    middle_len = MBTOK - head_len - tail_len
    return jnp.stack([head_len, middle_len, tail_len], axis=1).astype(jnp.int32)


def levels(rng, shape, cuts, least, largest):
    factor_of, own = 1.0, jax.random.fold_in(rng, 6)
    for position, blocks in cuts:
        heights = jnp.exp(jax.random.uniform(jax.random.fold_in(own, position), (blocks,), jnp.float32, least / len(cuts), largest / len(cuts)))
        factor_of = factor_of * jnp.repeat(heights, shape[position] // blocks).reshape([-1 if axis == position else 1 for axis in range(len(shape))])
    return factor_of


def normal_values(own_key, dims, spread, limit, cuts=(), kind=jnp.bfloat16):
    level = levels(own_key, dims, cuts, -0.22, 0.18) if cuts else 1.0
    drawn = jax.random.normal(own_key, dims, jnp.float32) * spread * level
    return jnp.minimum(jnp.maximum(drawn, -limit), limit).astype(kind)


def setup_inputs(seed: int = 0) -> dict:
    seeds = jax.random.split(jax.random.key(seed), 17)
    return {
        "tokens": normal_values(seeds[0], (BATCH, MBTOK, D), 1.0, 6.0, ((0, 8), (1, 8))),
        "cotangent": normal_values(seeds[1], (BATCH, MBTOK, D), 1.0, 6.0, ((0, 8), (1, 8)), jnp.float32),
        "lengths": draw_lengths(jax.random.fold_in(seeds[16], 71), 0),
        "ln1_gain": jnp.clip(1.0 + 0.1 * jax.random.normal(seeds[3], (2, D), jnp.float32), 0.5, 1.5).astype(jnp.bfloat16),
        "ln1_bias": normal_values(seeds[4], (2, D), 0.5, 3.0, ((0, 2), (1, 8))),
        "w_qkv": normal_values(seeds[5], (2, D, 3 * D), D ** -0.5, 0.21875, ((0, 2), (1, 8))),
        "b_query": normal_values(seeds[6], (2, D), 0.5, 3.0, ((0, 2), (1, 8))),
        "b_value": normal_values(seeds[7], (2, D), 0.5, 3.0, ((0, 2), (1, 8))),
        "w_out": normal_values(seeds[8], (2, D, D), (D // 16) ** -0.5, 0.875, ((0, 2), (1, 8))),
        "b_out": normal_values(seeds[9], (2, D), 0.5, 3.0, ((0, 2), (1, 8))),
        "ln2_gain": jnp.clip(1.0 + 0.1 * jax.random.normal(seeds[10], (2, D), jnp.float32), 0.5, 1.5).astype(jnp.bfloat16),
        "ln2_bias": normal_values(seeds[11], (2, D), 0.5, 3.0, ((0, 2), (1, 8))),
        "w_fc": normal_values(seeds[12], (2, D, FF), D ** -0.5, 0.21875, ((0, 2), (1, 8))),
        "b_fc": normal_values(seeds[13], (2, FF), 0.5, 3.0, ((0, 2), (1, 8))),
        "w_proj": normal_values(seeds[14], (2, FF, D), FF ** -0.5, 0.109375, ((0, 2), (1, 8))),
        "b_proj": normal_values(seeds[15], (2, D), 0.5, 3.0, ((0, 2), (1, 8))),
    }


@jax.custom_vjp
def low(v):
    return lax.optimization_barrier(v.astype(jnp.bfloat16)).astype(jnp.float32)

@jax.custom_vjp
def low_back(v):
    return v

def low_keep(v):
    return (low(v), None)

def low_pass(kept, grad):
    return (grad,)

def back_keep(v):
    return (v, None)

def back_low(kept, grad):
    return (low(grad),)
low.defvjp(low_keep, low_pass)
low_back.defvjp(back_keep, back_low)
EPSILON = 1e-05
HIGHEST = lax.Precision.HIGHEST

def layer_norm(inputs, gain, bias_term):
    center = inputs - lax.optimization_barrier(jnp.mean(inputs, axis=-1, keepdims=True))
    variance = lax.optimization_barrier(jnp.mean(center * center, axis=-1, keepdims=True))
    return center * lax.rsqrt(variance + EPSILON) * gain + bias_term

def document_ids(length_row, positions):
    first_end = length_row[0]
    second_end = first_end + length_row[1]
    return (positions >= first_end).astype(jnp.int32) + (positions >= second_end).astype(jnp.int32)

def attend(packed):
    queries, keys_all, values_all, length_row = packed
    positions = jnp.arange(MBTOK, dtype=jnp.int32)
    doc_ids = document_ids(length_row, positions)
    allowed = (doc_ids[:, None] == doc_ids[None, :]) & (positions[None, :] <= positions[:, None])
    query_heads = queries.reshape(MBTOK, HEADS, HEAD)
    key_heads = keys_all.reshape(MBTOK, HEADS, HEAD)
    value_heads = values_all.reshape(MBTOK, HEADS, HEAD)
    scores = jnp.einsum('qhd,khd->hqk', query_heads, key_heads, precision=HIGHEST)
    scores = low_back(scores) * 0.125
    scores = jnp.where(allowed[None], scores, -1e+30)
    maximum = lax.optimization_barrier(jnp.max(scores, axis=-1, keepdims=True))
    expo = jnp.exp(scores - maximum)
    probs = expo / lax.optimization_barrier(jnp.sum(expo, axis=-1, keepdims=True))
    mixed = jnp.einsum('hqk,khd->qhd', low(probs), value_heads, precision=HIGHEST)
    return low_back(mixed).reshape(MBTOK, D)

def layer(inputs, params, lengths):
    gain_one, bias_one, mat_qkv, bias_query, bias_value, mat_out, bias_out, gain_two, bias_two, mat_fc, bias_fc, mat_proj, bias_proj = params
    normed = layer_norm(inputs, gain_one, bias_one)
    projected = jnp.einsum('bsd,de->bse', low(normed), mat_qkv, precision=HIGHEST)
    queries = low(low_back(projected[..., :D] + bias_query))
    keys_all = low(low_back(projected[..., D:2 * D]))
    values_all = low(low_back(projected[..., 2 * D:] + bias_value))
    mixed = lax.map(jax.checkpoint(attend), (queries, keys_all, values_all, lengths))
    branch = low_back(jnp.einsum('bsd,de->bse', low(mixed), mat_out, precision=HIGHEST) + bias_out)
    middle = inputs + branch
    normed_two = layer_norm(middle, gain_two, bias_two)
    hidden_pre = low_back(jnp.einsum('bsd,df->bsf', low(normed_two), mat_fc, precision=HIGHEST) + bias_fc)
    active = jax.nn.gelu(hidden_pre, approximate=True)
    second_branch = low_back(jnp.einsum('bsf,fd->bsd', low(active), mat_proj, precision=HIGHEST) + bias_proj)
    return middle + second_branch

def forward(inputs, joint, params, lengths):
    first_out = low(layer(inputs, tuple((piece[0] for piece in params)), lengths))
    second_in = low_back(first_out) + joint
    second_out = layer(second_in, tuple((piece[1] for piece in params)), lengths)
    return (first_out, second_out)

def reference(tokens, cotangent, lengths, ln1_gain, ln1_bias, w_qkv, b_query, b_value, w_out, b_out, ln2_gain, ln2_bias, w_fc, b_fc, w_proj, b_proj):
    params = tuple((piece.astype(jnp.float32) for piece in (ln1_gain, ln1_bias, w_qkv, b_query, b_value, w_out, b_out, ln2_gain, ln2_bias, w_fc, b_fc, w_proj, b_proj)))
    inputs = tokens.astype(jnp.float32)
    joint = jnp.zeros_like(inputs)

    def whole(inputs_in, joint_in, params_in):
        return forward(inputs_in, joint_in, params_in, lengths)
    outputs, pullback = jax.vjp(whole, inputs, joint, params)
    grad_in, grad_joint, grad_params = pullback((jnp.zeros_like(inputs), cotangent.astype(jnp.float32)))
    acts = jnp.stack([outputs[0], outputs[1]]).astype(jnp.bfloat16)
    in_grads = jnp.stack([grad_in, grad_joint]).astype(jnp.bfloat16)
    return (acts, in_grads, grad_params[0], grad_params[1], grad_params[2], grad_params[3], grad_params[4], grad_params[5], grad_params[6], grad_params[7], grad_params[8], grad_params[9], grad_params[10], grad_params[11], grad_params[12])
```

```python
import functools

import jax
import jax.numpy as jnp
from jax import lax
from jax.experimental import pallas as pl
from jax.experimental.pallas import tpu as pltpu
from jax.sharding import PartitionSpec as P

WIDTH = 768
GROUPS = 8
PAIRS = 6
SEQ = 1024
ROWS = 128
BLOCK = 256
SHARD = 96
EPSILON = 1e-05
VMEM_BYTES = 40 * 1024 * 1024
GELU_C = 0.7978845608028654
BF = jnp.bfloat16
F32 = jnp.float32


def torus_pairs(move):
    pairs = []
    for source in range(64):
        group, replica = divmod(source, 8)
        x, z_lo = divmod(group, 2)
        z_hi, y = divmod(replica, 4)
        x, y, z = move(x, y, z_hi * 2 + z_lo)
        pairs.append((source, ((x % 4) * 2 + z % 2) * 8 + (z % 4) // 2 * 4 + y % 4))
    return pairs


def along_x(value, by):
    return lax.ppermute(value, ("group", "replica"), torus_pairs(lambda x, y, z: (x + by, y, z)))


def along_y(value, by):
    return lax.ppermute(value, ("group", "replica"), torus_pairs(lambda x, y, z: (x, y + by, z)))


def along_z(value, by):
    return lax.ppermute(value, ("group", "replica"), torus_pairs(lambda x, y, z: (x, y, z + by)))


def swap(value):
    return lax.ppermute(value, "section", [(0, 1), (1, 0)])


def gather_group(shard):
    group = lax.axis_index("group")
    x, z = group // 2, group % 2
    blocks = shard.shape[0]
    half = blocks // 2
    full = jnp.zeros((blocks, GROUPS) + shard.shape[1:], shard.dtype)

    def put(full, piece, dx, flip, first):
        at = lax.rem(x + dx + 4, 4) * 2 + (1 - z if flip else z)
        return lax.dynamic_update_slice(full, piece[:, None], (first, at, 0, 0))

    low, high = shard[:half], shard[half:]
    left = along_x(shard, 1)
    right = along_x(shard, -1)
    far_low = along_x(left[:half], 1)
    far_high = along_x(right[half:], -1)
    z_low = along_z(low, 1)
    z_high = along_z(high, -1)
    z_left = along_z(left, 1)
    z_right = along_z(right, -1)
    z_far_low = along_z(far_low, 1)
    z_far_high = along_z(far_high, -1)
    full = put(full, shard, 0, False, 0)
    full = put(full, left, -1, False, 0)
    full = put(full, right, 1, False, 0)
    full = put(full, far_low, 2, False, 0)
    full = put(full, far_high, 2, False, half)
    full = put(full, z_low, 0, True, 0)
    full = put(full, z_high, 0, True, half)
    full = put(full, z_left, -1, True, 0)
    full = put(full, z_right, 1, True, 0)
    full = put(full, z_far_low, 2, True, 0)
    full = put(full, z_far_high, 2, True, half)
    return full


def add(left, right):
    return left.astype(F32) + right.astype(F32)


def ring_sum(pieces, place, along):
    two = pieces(2)
    half = two.shape[0] // 2
    from_left = along(two[:half], 1)
    from_right = along(two[half:], -1)
    one, minus = pieces(1), pieces(3)
    one = jnp.concatenate([add(one[:half], from_left).astype(BF), one[half:]], axis=0)
    minus = jnp.concatenate([minus[:half], add(minus[half:], from_right).astype(BF)], axis=0)
    return pieces(0).astype(F32) + along(one, 1).astype(F32) + along(minus, -1).astype(F32)


def reduce_group(parts):
    group = lax.axis_index("group")
    x, z = group // 2, group % 2
    blocks, _, rows, width = parts.shape
    half = blocks // 2
    parts = parts.reshape(blocks, 4, 2, rows, width)
    away = lax.dynamic_index_in_dim(parts, 1 - z, 2, keepdims=False)
    own = lax.dynamic_index_in_dim(parts, z, 2, keepdims=False)
    low = add(own[:half], along_z(away[:half], 1)).astype(BF)
    high = add(own[half:], along_z(away[half:], -1)).astype(BF)
    own = jnp.concatenate([low, high], axis=0)

    def piece(k):
        return lax.dynamic_index_in_dim(own, lax.rem(x + k, 4), 1, keepdims=False)

    return ring_sum(piece, x, along_x)


def reduce_replica(total):
    y = lax.rem(lax.axis_index("replica"), 4)
    rows, width = total.shape
    quarter = rows // 4
    half = quarter // 2
    low = total.astype(BF)

    def piece(k):
        return lax.dynamic_slice(low, (lax.rem(y + k, 4) * quarter, 0), (quarter, width))

    mine = ring_sum(piece, y, along_y).astype(BF)
    mine = add(mine, along_z(mine, 2)).astype(BF)
    left = along_y(mine, 1)
    right = along_y(mine, -1)
    far_low = along_y(left[:half], 1)
    far_high = along_y(right[half:], -1)
    far = jnp.concatenate([far_low, far_high], axis=0)
    full = jnp.zeros((4, quarter, width), BF)
    for piece_k, k in ((mine, 0), (left, 3), (right, 1), (far, 2)):
        full = lax.dynamic_update_slice(full, piece_k[None], (lax.rem(y + k, 4), 0, 0))
    return full.reshape(rows, width)


def dot(left, right):
    return jnp.dot(left, right, preferred_element_type=F32)


def dot_rows(left, right):
    return lax.dot_general(left, right, (((0,), (0,)), ((), ())), preferred_element_type=F32)


def dot_columns(left, right):
    return lax.dot_general(left, right, (((1,), (1,)), ((), ())), preferred_element_type=F32)


def normalized(rows):
    center = rows - jnp.mean(rows, axis=-1, keepdims=True)
    scale = lax.rsqrt(jnp.mean(center * center, axis=-1, keepdims=True) + EPSILON)
    return center * scale, scale


def norm_back(grad, gain, unit, scale):
    inner = grad * gain
    return scale * (
        inner
        - jnp.mean(inner, axis=-1, keepdims=True)
        - unit * jnp.mean(inner * unit, axis=-1, keepdims=True)
    )


def column_sums(rows):
    return jnp.sum(rows, axis=0, keepdims=True)


def put_pairs(ref, rows, index=None):
    for pair in range(PAIRS):
        part = rows[:, pair * 128 : (pair + 1) * 128]
        if index is None:
            ref[pair] = part
        else:
            ref[pair, index] = part
    for pair in range(PAIRS, GROUPS):
        empty = jnp.zeros((ROWS, 128), BF)
        if index is None:
            ref[pair] = empty
        else:
            ref[pair, index] = empty


def pre_forward(x_ref, vec_ref, first_ref, value_ref, n1_ref, send_ref):
    unit, _ = normalized(x_ref[...].astype(F32))
    n1 = (unit * vec_ref[0:1, :] + vec_ref[1:2, :]).astype(BF)
    n1_ref[...] = n1
    put_pairs(send_ref, (dot(n1, first_ref[0]) + vec_ref[2:3, :]).astype(BF), 0)
    put_pairs(send_ref, dot(n1, first_ref[1]).astype(BF), 1)
    put_pairs(send_ref, (dot(n1, value_ref[0]) + vec_ref[3:4, :]).astype(BF), 2)


def visible(length_ref, at, columns):
    first_end = length_ref[0]
    second_end = first_end + length_ref[1]
    row = lax.broadcasted_iota(jnp.int32, (BLOCK, 1), 0) + at
    start = jnp.where(row >= second_end, second_end, jnp.where(row >= first_end, first_end, 0))
    column = lax.broadcasted_iota(jnp.int32, (BLOCK, columns), 1)
    return (column >= start) & (column <= row)


def of_head(rows, head):
    lane = lax.broadcasted_iota(jnp.int32, rows.shape, 1)
    keep = lane < 64 if head == 0 else lane >= 64
    return jnp.where(keep, rows, jnp.zeros_like(rows))


def both_heads(first, second):
    lane = lax.broadcasted_iota(jnp.int32, first.shape, 1)
    return jnp.where(lane < 64, first, second)


def attend_forward(length_ref, qkv_ref, out_ref, logsum_ref):
    for block in range(SEQ // BLOCK):
        keys = (block + 1) * BLOCK
        query = qkv_ref[2 * block : 2 * block + 2, 0].reshape(BLOCK, 128)
        query = (query.astype(F32) * 0.125).astype(BF)
        key = qkv_ref[: 2 * block + 2, 1].reshape(keys, 128)
        value = qkv_ref[: 2 * block + 2, 2].reshape(keys, 128)
        allowed = visible(length_ref, block * BLOCK, keys)
        mixed, sums = [], []
        for head in range(2):
            scores = dot_columns(of_head(query, head), key)
            scores = jnp.where(allowed, scores, -1e30)
            maximum = jnp.max(scores, axis=-1, keepdims=True)
            expo = jnp.exp(scores - maximum)
            total = jnp.sum(expo, axis=-1, keepdims=True)
            mixed.append(dot((expo * (1.0 / total)).astype(BF), value))
            sums.append(jnp.broadcast_to(maximum + jnp.log(total), (BLOCK, 128)))
        out_ref[2 * block : 2 * block + 2] = both_heads(*mixed).astype(BF).reshape(2, 128, 128)
        logsum_ref[block * BLOCK : (block + 1) * BLOCK, :] = both_heads(*sums)


def attend_backward(length_ref, qkv_ref, grad_ref, logsum_ref, out_ref, key_acc, value_acc):
    key_acc[...] = jnp.zeros_like(key_acc)
    value_acc[...] = jnp.zeros_like(value_acc)
    for block in range(SEQ // BLOCK):
        keys = (block + 1) * BLOCK
        query = qkv_ref[2 * block : 2 * block + 2, 0].reshape(BLOCK, 128)
        query = (query.astype(F32) * 0.125).astype(BF)
        grad = grad_ref[2 * block : 2 * block + 2].reshape(BLOCK, 128)
        key = qkv_ref[: 2 * block + 2, 1].reshape(keys, 128)
        value = qkv_ref[: 2 * block + 2, 2].reshape(keys, 128)
        allowed = visible(length_ref, block * BLOCK, keys)
        grad_query = []
        for head in range(2):
            query_one, grad_one = of_head(query, head), of_head(grad, head)
            logsum = logsum_ref[block * BLOCK : (block + 1) * BLOCK, 64 * head : 64 * head + 1]
            scores = jnp.where(allowed, dot_columns(query_one, key), -1e30)
            probs = jnp.exp(scores - logsum)
            grad_probs = dot_columns(grad_one, value)
            delta = jnp.sum(probs * grad_probs, axis=-1, keepdims=True)
            grad_scores = (probs * (grad_probs - delta)).astype(BF)
            grad_query.append(dot(grad_scores, key))
            key_acc[:keys, :] += dot_rows(grad_scores, query_one)
            value_acc[:keys, :] += dot_rows(probs.astype(BF), grad_one)
        out = (both_heads(*grad_query) * 0.125).astype(BF)
        out_ref[2 * block : 2 * block + 2, 0] = out.reshape(2, 128, 128)
    out_ref[:, 1] = key_acc[...].astype(BF).reshape(GROUPS, 128, 128)
    out_ref[:, 2] = value_acc[...].astype(BF).reshape(GROUPS, 128, 128)


def proj_block(proj_ref):
    return jnp.concatenate([proj_ref[j, g] for g in range(2) for j in range(4)], axis=0)


def post_forward(
    mixed_ref, x_ref, vec_ref, bias_ref, out_w_ref, fc_ref, proj_ref, y_ref, x1_ref, n2_ref, u_ref, acc
):
    step = pl.program_id(0)

    @pl.when(step == 0)
    def _():
        mixed = jnp.concatenate([mixed_ref[pair] for pair in range(PAIRS)], axis=1)
        x1 = x_ref[...].astype(F32) + dot(mixed, out_w_ref[0]) + vec_ref[4:5, :]
        x1_ref[...] = x1
        unit, _ = normalized(x1)
        n2_ref[...] = (unit * vec_ref[5:6, :] + vec_ref[6:7, :]).astype(BF)
        acc[...] = x1 + vec_ref[7:8, :]

    u = dot(n2_ref[...], fc_ref[0]) + bias_ref[0]
    u_ref[0] = u
    active = 0.5 * u * (1.0 + jnp.tanh(GELU_C * (u + 0.044715 * (u * u * u))))
    acc[...] += dot(active.astype(BF), proj_block(proj_ref))

    @pl.when(step == 3)
    def _():
        y_ref[...] = acc[...].astype(BF)


def post_backward(
    dy_ref,
    u_ref,
    n2_ref,
    x1_ref,
    mixed_ref,
    vec_ref,
    out_w_ref,
    fc_ref,
    proj_ref,
    dx1_ref,
    send_ref,
    dout_ref,
    dfc_ref,
    dproj_ref,
    dvec_ref,
    dbias_ref,
    acc,
):
    step = pl.program_id(0)
    dy = dy_ref[...].astype(F32)
    low = dy.astype(BF)

    @pl.when(step == 0)
    def _():
        acc[...] = jnp.zeros_like(acc)

    u = u_ref[0]
    square = u * u
    tanh = jnp.tanh(GELU_C * (u + 0.044715 * (square * u)))
    active = (0.5 * u * (1.0 + tanh)).astype(BF)
    slope = 0.5 * (1.0 + tanh) + 0.5 * u * (1.0 - tanh * tanh) * (
        GELU_C * (1.0 + 3.0 * 0.044715 * square)
    )
    du = (dot_columns(low, proj_block(proj_ref)) * slope).astype(BF)
    dproj = dot_rows(active, low).astype(BF)
    for g in range(2):
        for j in range(4):
            at = (g * 4 + j) * SHARD
            dproj_ref[j, g] = dproj[at : at + SHARD]
    dfc_ref[0] = dot_rows(n2_ref[...], du).astype(BF)
    dbias_ref[0] = column_sums(du.astype(F32))
    acc[...] += dot_columns(du, fc_ref[0])

    @pl.when(step == 3)
    def _():
        dn2 = acc[...]
        unit, scale = normalized(x1_ref[...])
        dx1 = dy + norm_back(dn2, vec_ref[5:6, :], unit, scale)
        dx1_ref[...] = dx1
        back = dx1.astype(BF)
        mixed = jnp.concatenate([mixed_ref[pair] for pair in range(PAIRS)], axis=1)
        dout_ref[...] = dot_rows(mixed, back).astype(BF)
        put_pairs(send_ref, dot_columns(back, out_w_ref[0]).astype(BF))
        dvec_ref[0:4, :] = jnp.zeros((4, WIDTH), F32)
        dvec_ref[4:5, :] = column_sums(back.astype(F32))
        dvec_ref[5:6, :] = column_sums(dn2 * unit)
        dvec_ref[6:7, :] = column_sums(dn2)
        dvec_ref[7:8, :] = column_sums(low.astype(F32))


def pre_backward(
    grads_ref, n1_ref, x_ref, dx1_ref, vec_ref, first_ref, value_ref, dx_ref, dfirst_ref, dvalue_ref, dvec_ref
):
    rows = [
        jnp.concatenate([grads_ref[pair, index] for pair in range(PAIRS)], axis=1)
        for index in range(3)
    ]
    n1 = n1_ref[...]
    dn1 = (
        dot_columns(rows[0], first_ref[0])
        + dot_columns(rows[1], first_ref[1])
        + dot_columns(rows[2], value_ref[0])
    )
    dfirst_ref[0] = dot_rows(n1, rows[0]).astype(BF)
    dfirst_ref[1] = dot_rows(n1, rows[1]).astype(BF)
    dvalue_ref[...] = dot_rows(n1, rows[2]).astype(BF)
    unit, scale = normalized(x_ref[...].astype(F32))
    dx_ref[...] = (dx1_ref[...] + norm_back(dn1, vec_ref[0:1, :], unit, scale)).astype(BF)
    dvec_ref[0:1, :] = column_sums(dn1 * unit)
    dvec_ref[1:2, :] = column_sums(dn1)
    dvec_ref[2:3, :] = column_sums(rows[0].astype(F32))
    dvec_ref[3:4, :] = column_sums(rows[2].astype(F32))
    dvec_ref[4:8, :] = jnp.zeros((4, WIDTH), F32)


def whole(*shape):
    return pl.BlockSpec(shape, lambda *_: (0,) * len(shape))


def stepped(*shape):
    return pl.BlockSpec(shape, lambda step: (step,) + (0,) * (len(shape) - 1))


def out(shape, kind):
    return jax.ShapeDtypeStruct(shape, kind)


def params():
    return pltpu.CompilerParams(vmem_limit_bytes=VMEM_BYTES)


def cost(us):
    return pl.CostEstimate(
        flops=int(us * 4e8), bytes_accessed=int(us * 3e6), transcendentals=0
    )


PROJ_SPEC = pl.BlockSpec((4, 2, SHARD, WIDTH), lambda step: (0, step, 0, 0))
SMEM_SPEC = pl.BlockSpec(memory_space=pltpu.SMEM)


def run_pre_forward(x, vec, first, second):
    return pl.pallas_call(
        pre_forward,
        grid=(1,),
        in_specs=[
            whole(ROWS, WIDTH),
            whole(8, WIDTH),
            whole(2, WIDTH, WIDTH),
            whole(1, WIDTH, WIDTH),
        ],
        out_specs=[whole(ROWS, WIDTH), whole(GROUPS, 3, ROWS, 128)],
        out_shape=[out((ROWS, WIDTH), BF), out((GROUPS, 3, ROWS, 128), BF)],
        compiler_params=params(),
        cost_estimate=cost(4),
        name="pre_forward",
    )(x, vec, first, second)


def run_attend_forward(length_row, qkv):
    return pl.pallas_call(
        attend_forward,
        grid=(1,),
        in_specs=[SMEM_SPEC, whole(GROUPS, 3, ROWS, 128)],
        out_specs=[whole(GROUPS, ROWS, 128), whole(SEQ, 128)],
        out_shape=[out((GROUPS, ROWS, 128), BF), out((SEQ, 128), F32)],
        compiler_params=params(),
        cost_estimate=cost(8),
        name="attend_forward",
    )(length_row, qkv)


def run_attend_backward(length_row, qkv, grad, logsum):
    return pl.pallas_call(
        attend_backward,
        grid=(1,),
        in_specs=[
            SMEM_SPEC,
            whole(GROUPS, 3, ROWS, 128),
            whole(GROUPS, ROWS, 128),
            whole(SEQ, 128),
        ],
        out_specs=whole(GROUPS, 3, ROWS, 128),
        out_shape=out((GROUPS, 3, ROWS, 128), BF),
        scratch_shapes=[pltpu.VMEM((SEQ, 128), F32), pltpu.VMEM((SEQ, 128), F32)],
        compiler_params=params(),
        cost_estimate=cost(16),
        name="attend_backward",
    )(length_row, qkv, grad, logsum)


def run_post_forward(mixed, x, vec, bias, second, fc, proj):
    return pl.pallas_call(
        post_forward,
        grid=(4,),
        in_specs=[
            whole(GROUPS, ROWS, 128),
            whole(ROWS, WIDTH),
            whole(8, WIDTH),
            stepped(1, 1, WIDTH),
            pl.BlockSpec((1, WIDTH, WIDTH), lambda step: (1, 0, 0)),
            stepped(1, WIDTH, WIDTH),
            PROJ_SPEC,
        ],
        out_specs=[
            whole(ROWS, WIDTH),
            whole(ROWS, WIDTH),
            whole(ROWS, WIDTH),
            stepped(1, ROWS, WIDTH),
        ],
        out_shape=[
            out((ROWS, WIDTH), BF),
            out((ROWS, WIDTH), F32),
            out((ROWS, WIDTH), BF),
            out((4, ROWS, WIDTH), F32),
        ],
        scratch_shapes=[pltpu.VMEM((ROWS, WIDTH), F32)],
        compiler_params=params(),
        cost_estimate=cost(8),
        name="post_forward",
    )(mixed, x, vec, bias, second, fc, proj)


def run_post_backward(dy, u, n2, x1, mixed, vec, second, fc, proj):
    return pl.pallas_call(
        post_backward,
        grid=(4,),
        in_specs=[
            whole(ROWS, WIDTH),
            stepped(1, ROWS, WIDTH),
            whole(ROWS, WIDTH),
            whole(ROWS, WIDTH),
            whole(GROUPS, ROWS, 128),
            whole(8, WIDTH),
            pl.BlockSpec((1, WIDTH, WIDTH), lambda step: (1, 0, 0)),
            stepped(1, WIDTH, WIDTH),
            PROJ_SPEC,
        ],
        out_specs=[
            whole(ROWS, WIDTH),
            whole(GROUPS, ROWS, 128),
            whole(WIDTH, WIDTH),
            stepped(1, WIDTH, WIDTH),
            PROJ_SPEC,
            whole(8, WIDTH),
            stepped(1, 1, WIDTH),
        ],
        out_shape=[
            out((ROWS, WIDTH), F32),
            out((GROUPS, ROWS, 128), BF),
            out((WIDTH, WIDTH), BF),
            out((4, WIDTH, WIDTH), BF),
            out((4, GROUPS, SHARD, WIDTH), BF),
            out((8, WIDTH), F32),
            out((4, 1, WIDTH), F32),
        ],
        scratch_shapes=[pltpu.VMEM((ROWS, WIDTH), F32)],
        compiler_params=params(),
        cost_estimate=cost(14),
        name="post_backward",
    )(dy, u, n2, x1, mixed, vec, second, fc, proj)


def run_pre_backward(grads, n1, x, dx1, vec, first, second):
    return pl.pallas_call(
        pre_backward,
        grid=(1,),
        in_specs=[
            whole(GROUPS, 3, ROWS, 128),
            whole(ROWS, WIDTH),
            whole(ROWS, WIDTH),
            whole(ROWS, WIDTH),
            whole(8, WIDTH),
            whole(2, WIDTH, WIDTH),
            whole(1, WIDTH, WIDTH),
        ],
        out_specs=[
            whole(ROWS, WIDTH),
            whole(2, WIDTH, WIDTH),
            whole(WIDTH, WIDTH),
            whole(8, WIDTH),
        ],
        out_shape=[
            out((ROWS, WIDTH), BF),
            out((2, WIDTH, WIDTH), BF),
            out((WIDTH, WIDTH), BF),
            out((8, WIDTH), F32),
        ],
        compiler_params=params(),
        cost_estimate=cost(8),
        name="pre_backward",
    )(grads, n1, x, dx1, vec, first, second)


def exchange(value):
    return lax.all_to_all(value, "group", 0, 0, tiled=True)


def body(
    tokens,
    cotangent,
    lengths,
    ln1_gain,
    ln1_bias,
    w_qkv,
    b_query,
    b_value,
    w_out,
    b_out,
    ln2_gain,
    ln2_bias,
    w_fc,
    b_fc,
    w_proj,
    b_proj,
):
    section = lax.axis_index("section")
    group = lax.axis_index("group")

    def pick(on_first, on_second):
        return jnp.where(section == 0, on_first, on_second)

    def ordered(mine, other):
        return pick(mine, other), pick(other, mine)

    qkv = w_qkv[0].reshape(SHARD, 3, WIDTH).transpose(1, 0, 2)
    fc = w_fc[0].reshape(SHARD, 4, WIDTH).transpose(1, 0, 2)
    half_a = jnp.concatenate([qkv[:2], fc], axis=0)
    half_b = jnp.concatenate([qkv[2:], w_out, w_proj[0].reshape(4, SHARD, WIDTH)], axis=0)
    got = swap(pick(half_b, half_a))
    shard_zero, shard_one = pick(half_a, got), pick(got, half_b)

    vectors = jnp.concatenate(
        [ln1_gain, ln1_bias, b_query, b_value, b_out, ln2_gain, ln2_bias, b_proj, b_fc.reshape(4, SHARD)],
        axis=0,
    )
    vectors = jnp.concatenate(ordered(vectors, swap(vectors)), axis=0)
    vectors = lax.all_gather(vectors, "group", axis=0).astype(F32)

    def vector_rows(layer):
        own = vectors[:, 12 * layer : 12 * layer + 12]
        rows = own[:, :8].transpose(1, 0, 2).reshape(8, WIDTH)
        return rows, own[:, 8:].reshape(4, 1, WIDTH)

    def both_halves(shard):
        mine = gather_group(shard)
        return ordered(mine, swap(mine))

    def gather_layer(shard):
        first, second = both_halves(shard[:2])
        wide, proj = both_halves(shard[2:])
        return (
            first.reshape(2, WIDTH, WIDTH),
            second.reshape(2, WIDTH, WIDTH),
            wide.reshape(4, WIDTH, WIDTH),
            proj,
        )

    weights = (gather_layer(shard_zero), gather_layer(shard_one))
    length_row = lax.dynamic_index_in_dim(lengths, section, 0, keepdims=False)
    rows = lax.dynamic_index_in_dim(tokens, section, 0, keepdims=False)

    outputs, kept = [], []
    for layer in range(2):
        first, second, wide, proj = weights[layer]
        vec, bias = vector_rows(layer)
        n1, send = run_pre_forward(rows, vec, first, second)
        heads = exchange(send)
        mixed, logsum = run_attend_forward(length_row, heads)
        mixed = exchange(mixed)
        result, x1, n2, u = run_post_forward(mixed, rows, vec, bias, second, wide, proj)
        kept.append((rows, vec, n1, heads, logsum, mixed, x1, n2, u))
        outputs.append(result)
        rows = result

    grad = lax.dynamic_index_in_dim(cotangent, section, 0, keepdims=False)
    grads_in, sums_vec, sums = [None, None], [None, None], [None, None]
    for layer in (1, 0):
        first, second, wide, proj = weights[layer]
        rows, vec, n1, heads, logsum, mixed, x1, n2, u = kept[layer]
        dx1, send, dout, dwide, dproj, dvec_two, dbias = run_post_backward(
            grad, u, n2, x1, mixed, vec, second, wide, proj
        )
        dwide = dwide.reshape(4, GROUPS, SHARD, WIDTH)
        arrived = swap(pick(dproj, dwide))
        part = add(pick(dwide, dproj), arrived).astype(BF)
        wide_sum = reduce_group(part)
        wide_sum = reduce_replica(wide_sum.reshape(4 * SHARD, WIDTH))
        grad_heads = exchange(send)
        dheads = run_attend_backward(length_row, heads, grad_heads, logsum)
        dheads = exchange(dheads)
        grad, dfirst, dvalue, dvec_one = run_pre_backward(dheads, n1, rows, dx1, vec, first, second)
        grads_in[layer] = grad
        dsecond = jnp.stack([dvalue, dout])
        arrived = swap(pick(dsecond, dfirst))
        part = add(pick(dfirst, dsecond), arrived).astype(BF).reshape(2, GROUPS, SHARD, WIDTH)
        dvec = jnp.concatenate([dvec_one + dvec_two, dbias.reshape(4, WIDTH)], axis=0)
        sums_vec[layer] = dvec
        extra = 0
        if layer == 0:
            vecs = jnp.stack(sums_vec)
            vecs = vecs + swap(vecs)
            plain = vecs[:, :8].reshape(2, 8, GROUPS, SHARD).transpose(2, 0, 1, 3)
            bias = vecs[:, 8:].reshape(2, GROUPS, 4, SHARD).transpose(1, 0, 2, 3)
            packed = jnp.concatenate([plain, bias], axis=2).reshape(GROUPS, 3, WIDTH).astype(BF)
            extra = 16
            packed = jnp.pad(packed[None], ((0, 1), (0, 0), (0, extra - 3), (0, 0)))
            part = jnp.concatenate([part, packed], axis=2)
        slim = reduce_group(part)
        slim = reduce_replica(slim.reshape(2 * (SHARD + extra), WIDTH))
        slim = slim.reshape(2, SHARD + extra, WIDTH)
        if layer == 0:
            vec_sums = slim[0, SHARD : SHARD + 3].reshape(2, 12, SHARD)
        sums[layer] = (slim[:, :SHARD], wide_sum.reshape(4, SHARD, WIDTH))

    def own_layer(zero, one):
        mine, other = pick(zero, one), swap(pick(one, zero))
        first, second = ordered(mine, other)
        return first.astype(F32), second.astype(F32)

    both = [jnp.concatenate(sums[layer], axis=0) for layer in range(2)]
    first, second = own_layer(*both)
    grad_qkv = jnp.concatenate([first[0], first[1], second[0]], axis=1)
    grad_out = second[1]
    grad_fc = first[2:].transpose(1, 0, 2).reshape(SHARD, 4 * WIDTH)
    grad_proj = second[2:].reshape(4 * SHARD, WIDTH)
    vec_sums = pick(vec_sums[0], vec_sums[1]).astype(F32)

    def both_micro(zero, one):
        mine, other = pick(zero, one), swap(pick(one, zero))
        return jnp.stack(ordered(mine, other))[None]

    acts = both_micro(*outputs)
    in_grads = both_micro(*grads_in)
    v = vec_sums
    return (
        acts,
        in_grads,
        v[0:1],
        v[1:2],
        grad_qkv[None],
        v[2:3],
        v[3:4],
        grad_out[None],
        v[4:5],
        v[5:6],
        v[6:7],
        grad_fc[None],
        v[8:12].reshape(1, 4 * SHARD),
        grad_proj[None],
        v[7:8],
    )


def solution(mesh):
    placed = (
        P("replica", "group", None),
        P("replica", "group", None),
        P("replica", None),
        P("section", "group"),
        P("section", "group"),
        P("section", "group", None),
        P("section", "group"),
        P("section", "group"),
        P("section", "group", None),
        P("section", "group"),
        P("section", "group"),
        P("section", "group"),
        P("section", "group", None),
        P("section", "group"),
        P("section", "group", None),
        P("section", "group"),
    )
    return jax.shard_map(
        body,
        mesh=mesh,
        in_specs=placed,
        out_specs=(
            P("section", "replica", "group", None),
            P("section", "replica", "group", None),
            P("section", "group"),
            P("section", "group"),
            P("section", "group", None),
            P("section", "group"),
            P("section", "group"),
            P("section", "group", None),
            P("section", "group"),
            P("section", "group"),
            P("section", "group"),
            P("section", "group", None),
            P("section", "group"),
            P("section", "group", None),
            P("section", "group"),
        ),
        check_vma=False,
    )
```

```python
import functools

import jax
import jax.numpy as jnp
from jax import lax
from jax.experimental import pallas as pl
from jax.experimental.pallas import tpu as pltpu
from jax.sharding import PartitionSpec as P

WIDTH = 768
GROUPS = 8
PAIRS = 6
SEQ = 1024
ROWS = 128
BLOCK = 256
SHARD = 96
HALF = 48
SLIM = 192
WIDE = 384
VEC_ROWS = 16
EPSILON = 1e-05
VMEM_BYTES = 40 * 1024 * 1024
GELU_C = 0.7978845608028654
BF = jnp.bfloat16
F32 = jnp.float32


def torus_pairs(move):
    pairs = []
    for source in range(64):
        group, replica = divmod(source, 8)
        x, z_lo = divmod(group, 2)
        z_hi, y = divmod(replica, 4)
        x, y, z = move(x, y, z_hi * 2 + z_lo)
        pairs.append((source, ((x % 4) * 2 + z % 2) * 8 + (z % 4) // 2 * 4 + y % 4))
    return pairs


def along_x(value, by):
    return lax.ppermute(value, ("group", "replica"), torus_pairs(lambda x, y, z: (x + by, y, z)))


def along_y(value, by):
    return lax.ppermute(value, ("group", "replica"), torus_pairs(lambda x, y, z: (x, y + by, z)))


def along_z(value, by):
    return lax.ppermute(value, ("group", "replica"), torus_pairs(lambda x, y, z: (x, y, z + by)))


def swap(value):
    return lax.ppermute(value, "section", [(0, 1), (1, 0)])


def tie(*values):
    return lax.optimization_barrier(values)


def pick(on_first, on_second):
    return jnp.where(lax.axis_index("section") == 0, on_first, on_second)


class Gather:
    def __init__(self, shard):
        self.shard = shard
        self.cut = shard.shape[0] // 2

    def near(self):
        shard, cut = self.shard, self.cut
        self.left = along_x(shard, 1)
        self.right = along_x(shard, -1)
        self.z_low = along_z(shard[:cut], 1)
        self.z_high = along_z(shard[cut:], -1)

    def far(self):
        cut = self.cut
        self.far_low = along_x(self.left[:cut], 1)
        self.far_high = along_x(self.right[cut:], -1)
        self.z_left = along_z(self.left, 1)
        self.z_right = along_z(self.right, -1)

    def last(self):
        self.z_far_low = along_z(self.far_low, 1)
        self.z_far_high = along_z(self.far_high, -1)

    def after(self, *values):
        names = [name for name in vars(self) if name not in ("cut",)]
        count = len(names)
        tied = tie(*(getattr(self, name) for name in names), *values)
        for name, value in zip(names, tied):
            setattr(self, name, value)
        return tied[count:] if len(values) != 1 else tied[count]

    def whole(self):
        pieces = (
            self.shard,
            self.left,
            self.right,
            self.far_low,
            self.far_high,
            self.z_low,
            self.z_high,
            self.z_left,
            self.z_right,
            self.z_far_low,
            self.z_far_high,
        )
        return assemble(self.cut, *pieces)


def add(left, right):
    return left.astype(F32) + right.astype(F32)


class GroupSum:
    def __init__(self, pairs):
        self.own, away_low, away_high = sum_pairs(pairs)
        self.low = along_z(away_low, 1)
        self.high = along_z(away_high, -1)

    def far(self):
        self.zero, self.one, self.minus, two_low, two_high = sum_z(self.own, self.low, self.high)
        self.from_left = along_x(two_low, 1)
        self.from_right = along_x(two_high, -1)

    def near(self):
        one, minus = sum_far(self.one, self.minus, self.from_left, self.from_right)
        self.one = along_x(one, 1)
        self.minus = along_x(minus, -1)

    def total(self):
        return self.zero.astype(F32) + self.one.astype(F32) + self.minus.astype(F32)


class RingSum:
    def __init__(self, parts, place, along):
        self.parts, self.place, self.along = parts, place, along
        self.cut = parts.shape[1] // 2

    def piece(self, k):
        return lax.dynamic_index_in_dim(self.parts, lax.rem(self.place + k, 4), 0, keepdims=False)

    def far(self):
        two, cut = self.piece(2), self.cut
        self.from_left = self.along(two[:cut], 1)
        self.from_right = self.along(two[cut:], -1)

    def near(self):
        one, minus, cut = self.piece(1), self.piece(3), self.cut
        one = jnp.concatenate([add(one[:cut], self.from_left).astype(BF), one[cut:]], axis=0)
        minus = jnp.concatenate([minus[:cut], add(minus[cut:], self.from_right).astype(BF)], axis=0)
        self.one = self.along(one, 1)
        self.minus = self.along(minus, -1)

    def total(self):
        return self.piece(0).astype(F32) + self.one.astype(F32) + self.minus.astype(F32)


def over_replica(total):
    y = lax.rem(lax.axis_index("replica"), 4)
    rows, width = total.shape
    quarter = rows // 4
    half = quarter // 2
    ring = RingSum(total.astype(BF).reshape(4, quarter, width), y, along_y)
    ring.far()
    ring.near()
    mine = ring.total().astype(BF)
    mine = add(mine, along_z(mine, 2)).astype(BF)
    left = along_y(mine, 1)
    right = along_y(mine, -1)
    far = jnp.concatenate([along_y(left[:half], 1), along_y(right[half:], -1)], axis=0)
    full = jnp.zeros((4, quarter, width), BF)
    for piece, k in ((mine, 0), (left, 3), (right, 1), (far, 2)):
        full = lax.dynamic_update_slice(full, piece[None], (lax.rem(y + k, 4), 0, 0))
    return full.reshape(rows, width)


def over_all(parts):
    _, rows, width = parts.shape
    piece = rows // 8
    arrived = lax.all_to_all(parts.reshape(64, piece, width), ("group", "replica"), 0, 0, tiled=True)
    mine = jnp.sum(arrived.astype(F32), axis=0).astype(BF)
    spread = jnp.broadcast_to(mine[None], (8, piece, width))
    return lax.all_to_all(spread, "replica", 0, 0, tiled=True).reshape(rows, width)


def dot(left, right):
    return jnp.dot(left, right, preferred_element_type=F32)


def dot_rows(left, right):
    return lax.dot_general(left, right, (((0,), (0,)), ((), ())), preferred_element_type=F32)


def dot_columns(left, right):
    return lax.dot_general(left, right, (((1,), (1,)), ((), ())), preferred_element_type=F32)


def normalized(rows):
    center = rows - jnp.mean(rows, axis=-1, keepdims=True)
    scale = lax.rsqrt(jnp.mean(center * center, axis=-1, keepdims=True) + EPSILON)
    return center * scale, scale


def norm_back(grad, gain, unit, scale):
    inner = grad * gain
    return scale * (
        inner
        - jnp.mean(inner, axis=-1, keepdims=True)
        - unit * jnp.mean(inner * unit, axis=-1, keepdims=True)
    )


def column_sums(rows):
    return jnp.sum(rows, axis=0, keepdims=True)


PLACES = (
    (0, False, False),
    (3, False, False),
    (1, False, False),
    (2, False, False),
    (2, False, True),
    (0, True, False),
    (0, True, True),
    (3, True, False),
    (1, True, False),
    (2, True, False),
    (2, True, True),
)


def assemble_rows(cut, *refs):
    pieces, full = refs[: len(PLACES)], refs[len(PLACES)]
    group = lax.axis_index("group")
    x, z = group // 2, group % 2
    for piece, (dx, flip, high) in zip(pieces, PLACES):
        at = lax.rem(x + dx, 4) * 2 + (1 - z if flip else z)
        row = cut if high else 0
        full[pl.ds(at, 1), row : row + piece.shape[0]] = piece[...][None]


def assemble(cut, *pieces):
    rows = pieces[0].shape[0]
    return pl.pallas_call(
        functools.partial(assemble_rows, cut),
        in_specs=[pl.BlockSpec(memory_space=pltpu.VMEM)] * len(PLACES),
        out_specs=pl.BlockSpec(memory_space=pltpu.VMEM),
        out_shape=jax.ShapeDtypeStruct((GROUPS, rows, WIDTH), BF),
        compiler_params=pltpu.CompilerParams(vmem_limit_bytes=VMEM_BYTES),
        cost_estimate=cost(4),
        name="assemble",
    )(*pieces)


def pack_shard(section_ref, qkv_ref, out_ref, fc_ref, proj_ref, bias_ref, *refs):
    vectors, (keep_ref, away_ref) = refs[:8], refs[8:]
    on_first = section_ref[0] == 0

    def put(row, low, high):
        at = slice(row, row + low.shape[0])
        keep_ref[at, :] = lax.select(on_first, low, high)
        away_ref[at, :] = lax.select(on_first, high, low)

    for j in range(3):
        at = slice(WIDTH * j, WIDTH * (j + 1))
        put(HALF * j, qkv_ref[0, :HALF, at], qkv_ref[0, HALF:, at])
    put(3 * HALF, out_ref[0, :HALF], out_ref[0, HALF:])
    for j in range(4):
        at = slice(WIDTH * j, WIDTH * (j + 1))
        put(SLIM + VEC_ROWS + HALF * j, fc_ref[0, :HALF, at], fc_ref[0, HALF:, at])
    put(SLIM + VEC_ROWS + 4 * HALF, proj_ref[0, : 4 * HALF], proj_ref[0, 4 * HALF :])
    rows = jnp.concatenate([ref[...].astype(F32) for ref in vectors], axis=0)
    rows = jnp.concatenate([rows, jnp.zeros((8, WIDTH - SHARD), F32)], axis=1)
    bias = jnp.concatenate([bias_ref[...].astype(F32), jnp.zeros((1, WIDTH // 2), F32)], axis=1)
    rows = jnp.concatenate([rows, bias, jnp.zeros((7, WIDTH), F32)], axis=0).astype(BF)
    put(SLIM, rows, rows)


def run_pack_shard(section, qkv, out_w, fc, proj, bias, *vectors):
    vmem = pl.BlockSpec(memory_space=pltpu.VMEM)
    shape = jax.ShapeDtypeStruct((SLIM + VEC_ROWS + WIDE, WIDTH), BF)
    return pl.pallas_call(
        pack_shard,
        in_specs=[pl.BlockSpec(memory_space=pltpu.SMEM)] + [vmem] * 13,
        out_specs=[vmem, vmem],
        out_shape=[shape, shape],
        compiler_params=pltpu.CompilerParams(vmem_limit_bytes=VMEM_BYTES),
        cost_estimate=cost(3),
        name="pack_shard",
    )(section, qkv, out_w, fc, proj, bias, *vectors)


def one_hot(group):
    row = lax.broadcasted_iota(jnp.int32, (128, WIDTH), 0)
    lane = lax.broadcasted_iota(jnp.int32, (128, WIDTH), 1)
    return jnp.where((lane == row + SHARD * group) & (row < SHARD), 1.0, 0.0).astype(BF)


def unpack_vectors(mine_ref, vecs_ref):
    total = jnp.zeros((2 * VEC_ROWS, WIDTH), F32)
    for group in range(GROUPS):
        total = total + dot(mine_ref[group, :, :128], one_hot(group))
    for layer in range(2):
        vecs_ref[layer, 0:8, :] = total[VEC_ROWS * layer : VEC_ROWS * layer + 8]
        for j in range(4):
            for side in range(2):
                piece = mine_ref[2 * j + side, VEC_ROWS * layer : VEC_ROWS * (layer + 1), : WIDTH // 2]
                at = slice(side * (WIDTH // 2), (side + 1) * (WIDTH // 2))
                vecs_ref[layer, 8 + j : 9 + j, at] = piece.astype(F32)[8:9]


def run_unpack_vectors(mine):
    return pl.pallas_call(
        unpack_vectors,
        grid=(1,),
        in_specs=[pl.BlockSpec((GROUPS, 2 * VEC_ROWS, WIDTH), lambda step: (0, SLIM // (2 * VEC_ROWS), 0))],
        out_specs=whole(2, 12, WIDTH),
        out_shape=jax.ShapeDtypeStruct((2, 12, WIDTH), F32),
        cost_estimate=cost(2),
        name="unpack_vectors",
    )(mine)


def pack_vectors(vecs_ref, out_ref):
    for group in range(GROUPS):
        for layer in range(2):
            rows = lax.dot_general(
                vecs_ref[layer, 0:8, :].astype(BF),
                one_hot(group),
                (((1,), (1,)), ((), ())),
                preferred_element_type=F32,
            )
            rows = jnp.concatenate([rows, jnp.zeros((8, WIDTH - 128), F32)], axis=1)
            side = group % 2
            at = slice(side * (WIDTH // 2), (side + 1) * (WIDTH // 2))
            bias = vecs_ref[layer, 8 + group // 2 : 9 + group // 2, at]
            bias = jnp.concatenate([bias, jnp.zeros((1, WIDTH // 2), F32)], axis=1)
            rows = jnp.concatenate([rows, bias, jnp.zeros((7, WIDTH), F32)], axis=0)
            out_ref[group, VEC_ROWS * layer : VEC_ROWS * (layer + 1)] = rows.astype(BF)


def run_pack_vectors(vecs):
    return pl.pallas_call(
        pack_vectors,
        grid=(1,),
        in_specs=[whole(2, 12, WIDTH)],
        out_specs=whole(GROUPS, 2 * VEC_ROWS, WIDTH),
        out_shape=jax.ShapeDtypeStruct((GROUPS, 2 * VEC_ROWS, WIDTH), BF),
        cost_estimate=cost(2),
        name="pack_vectors",
    )(vecs)


def put_pairs(ref, rows, *index):
    for pair in range(PAIRS):
        ref[(pair, *index)] = rows[:, pair * 128 : (pair + 1) * 128]
    for pair in range(PAIRS, GROUPS):
        ref[(pair, *index)] = jnp.zeros((ROWS, 128), BF)


def weave(section_ref, mine_ref, other_ref):
    on_first = section_ref[0] == 0
    mine, other = mine_ref[...], other_ref[...]
    both = [lax.select(on_first, mine, other), lax.select(on_first, other, mine)]
    return jnp.concatenate(both, axis=1).reshape(WIDTH, WIDTH)


def unweave(section_ref, rows, keep_ref, away_ref):
    on_first = section_ref[0] == 0
    groups, half, _ = keep_ref.shape
    rows = rows.reshape(groups, 2 * half, WIDTH)
    low, high = rows[:, :half], rows[:, half:]
    keep_ref[...] = lax.select(on_first, low, high)
    away_ref[...] = lax.select(on_first, high, low)


def pre_forward(section_ref, x_ref, vec_ref, mine_ref, other_ref, n1_ref, send_ref):
    step = pl.program_id(0)

    @pl.when(step == 0)
    def _():
        unit, _ = normalized(x_ref[...].astype(F32))
        n1_ref[...] = (unit * vec_ref[0:1, :] + vec_ref[1:2, :]).astype(BF)

    bias = jnp.where(step == 0, vec_ref[2:3, :], jnp.where(step == 2, vec_ref[3:4, :], 0.0))
    product = dot(n1_ref[...], weave(section_ref, mine_ref, other_ref))
    put_pairs(send_ref, (product + bias).astype(BF), 0)


def visible(length_ref, at, columns):
    first_end = length_ref[0]
    second_end = first_end + length_ref[1]
    row = lax.broadcasted_iota(jnp.int32, (BLOCK, 1), 0) + at
    start = jnp.where(row >= second_end, second_end, jnp.where(row >= first_end, first_end, 0))
    column = lax.broadcasted_iota(jnp.int32, (BLOCK, columns), 1)
    return (column >= start) & (column <= row)


def of_head(rows, head):
    lane = lax.broadcasted_iota(jnp.int32, rows.shape, 1)
    keep = lane < 64 if head == 0 else lane >= 64
    return jnp.where(keep, rows, jnp.zeros_like(rows))


def both_heads(first, second):
    lane = lax.broadcasted_iota(jnp.int32, first.shape, 1)
    return jnp.where(lane < 64, first, second)


def attend_forward(length_ref, qkv_ref, out_ref, logsum_ref):
    for block in range(SEQ // BLOCK):
        keys = (block + 1) * BLOCK
        query = qkv_ref[2 * block : 2 * block + 2, 0].reshape(BLOCK, 128)
        query = (query.astype(F32) * 0.125).astype(BF)
        key = qkv_ref[: 2 * block + 2, 1].reshape(keys, 128)
        value = qkv_ref[: 2 * block + 2, 2].reshape(keys, 128)
        allowed = visible(length_ref, block * BLOCK, keys)
        mixed, sums = [], []
        for head in range(2):
            scores = dot_columns(of_head(query, head), key)
            scores = jnp.where(allowed, scores, -1e30)
            maximum = jnp.max(scores, axis=-1, keepdims=True)
            expo = jnp.exp(scores - maximum)
            total = jnp.sum(expo, axis=-1, keepdims=True)
            mixed.append(dot((expo * (1.0 / total)).astype(BF), value))
            sums.append(jnp.broadcast_to(maximum + jnp.log(total), (BLOCK, 128)))
        out_ref[2 * block : 2 * block + 2] = both_heads(*mixed).astype(BF).reshape(2, 128, 128)
        logsum_ref[block * BLOCK : (block + 1) * BLOCK, :] = both_heads(*sums)


def attend_backward(length_ref, qkv_ref, grad_ref, logsum_ref, out_ref, key_acc, value_acc):
    key_acc[...] = jnp.zeros_like(key_acc)
    value_acc[...] = jnp.zeros_like(value_acc)
    for block in range(SEQ // BLOCK):
        keys = (block + 1) * BLOCK
        query = qkv_ref[2 * block : 2 * block + 2, 0].reshape(BLOCK, 128)
        query = (query.astype(F32) * 0.125).astype(BF)
        grad = grad_ref[2 * block : 2 * block + 2].reshape(BLOCK, 128)
        key = qkv_ref[: 2 * block + 2, 1].reshape(keys, 128)
        value = qkv_ref[: 2 * block + 2, 2].reshape(keys, 128)
        allowed = visible(length_ref, block * BLOCK, keys)
        grad_query = []
        for head in range(2):
            query_one, grad_one = of_head(query, head), of_head(grad, head)
            logsum = logsum_ref[block * BLOCK : (block + 1) * BLOCK, 64 * head : 64 * head + 1]
            scores = jnp.where(allowed, dot_columns(query_one, key), -1e30)
            probs = jnp.exp(scores - logsum)
            grad_probs = dot_columns(grad_one, value)
            delta = jnp.sum(probs * grad_probs, axis=-1, keepdims=True)
            grad_scores = (probs * (grad_probs - delta)).astype(BF)
            grad_query.append(dot(grad_scores, key))
            key_acc[:keys, :] += dot_rows(grad_scores, query_one)
            value_acc[:keys, :] += dot_rows(probs.astype(BF), grad_one)
        out = (both_heads(*grad_query) * 0.125).astype(BF)
        out_ref[2 * block : 2 * block + 2, 0] = out.reshape(2, 128, 128)
    out_ref[:, 1] = key_acc[...].astype(BF).reshape(GROUPS, 128, 128)
    out_ref[:, 2] = value_acc[...].astype(BF).reshape(GROUPS, 128, 128)


def post_forward(
    section_ref,
    mixed_ref,
    x_ref,
    vec_ref,
    out_mine,
    out_other,
    fc_mine,
    fc_other,
    proj_mine,
    proj_other,
    y_ref,
    x1_ref,
    n2_ref,
    u_ref,
    acc,
):
    step = pl.program_id(0)

    @pl.when(step == 0)
    def _():
        mixed = jnp.concatenate([mixed_ref[pair] for pair in range(PAIRS)], axis=1)
        x1 = x_ref[...].astype(F32) + dot(mixed, weave(section_ref, out_mine, out_other))
        x1 = x1 + vec_ref[4:5, :]
        x1_ref[...] = x1
        unit, _ = normalized(x1)
        n2_ref[...] = (unit * vec_ref[5:6, :] + vec_ref[6:7, :]).astype(BF)
        acc[...] = x1 + vec_ref[7:8, :]

    u = dot(n2_ref[...], weave(section_ref, fc_mine, fc_other)) + vec_ref[pl.ds(8 + step, 1), :]
    u_ref[0] = u
    active = 0.5 * u * (1.0 + jnp.tanh(GELU_C * (u + 0.044715 * (u * u * u))))
    acc[...] += dot(active.astype(BF), weave(section_ref, proj_mine, proj_other))

    @pl.when(step == 3)
    def _():
        y_ref[...] = acc[...].astype(BF)


def post_backward(
    section_ref,
    dy_ref,
    u_ref,
    n2_ref,
    x1_ref,
    mixed_ref,
    vec_ref,
    out_mine,
    out_other,
    fc_mine,
    fc_other,
    proj_mine,
    proj_other,
    dx1_ref,
    send_ref,
    dvec_ref,
    dout_keep,
    dout_away,
    dfc_keep,
    dfc_away,
    dproj_keep,
    dproj_away,
    acc,
):
    step = pl.program_id(0)
    dy = dy_ref[...].astype(F32)
    low = dy.astype(BF)

    @pl.when(step == 0)
    def _():
        acc[...] = jnp.zeros_like(acc)

    u = u_ref[0]
    square = u * u
    tanh = jnp.tanh(GELU_C * (u + 0.044715 * (square * u)))
    active = (0.5 * u * (1.0 + tanh)).astype(BF)
    slope = 0.5 * (1.0 + tanh) + 0.5 * u * (1.0 - tanh * tanh) * (
        GELU_C * (1.0 + 3.0 * 0.044715 * square)
    )
    du = (dot_columns(low, weave(section_ref, proj_mine, proj_other)) * slope).astype(BF)
    unweave(section_ref, dot_rows(active, low).astype(BF), dproj_keep, dproj_away)
    unweave(section_ref, dot_rows(n2_ref[...], du).astype(BF), dfc_keep, dfc_away)
    dvec_ref[pl.ds(8 + step, 1), :] = column_sums(du.astype(F32))
    acc[...] += dot_columns(du, weave(section_ref, fc_mine, fc_other))

    @pl.when(step == 3)
    def _():
        dn2 = acc[...]
        unit, scale = normalized(x1_ref[...])
        dx1 = dy + norm_back(dn2, vec_ref[5:6, :], unit, scale)
        dx1_ref[...] = dx1
        back = dx1.astype(BF)
        mixed = jnp.concatenate([mixed_ref[pair] for pair in range(PAIRS)], axis=1)
        unweave(section_ref, dot_rows(mixed, back).astype(BF), dout_keep, dout_away)
        put_pairs(send_ref, dot_columns(back, weave(section_ref, out_mine, out_other)).astype(BF))
        dvec_ref[0:4, :] = jnp.zeros((4, WIDTH), F32)
        dvec_ref[4:5, :] = column_sums(back.astype(F32))
        dvec_ref[5:6, :] = column_sums(dn2 * unit)
        dvec_ref[6:7, :] = column_sums(dn2)
        dvec_ref[7:8, :] = column_sums(low.astype(F32))


def pre_backward(
    section_ref,
    grads_ref,
    n1_ref,
    x_ref,
    dx1_ref,
    vec_ref,
    mine_ref,
    other_ref,
    dx_ref,
    dvec_ref,
    keep_ref,
    away_ref,
    acc,
):
    step = pl.program_id(0)

    @pl.when(step == 0)
    def _():
        acc[...] = jnp.zeros_like(acc)
        dvec_ref[...] = jnp.zeros_like(dvec_ref)

    rows = jnp.concatenate([grads_ref[pair, 0] for pair in range(PAIRS)], axis=1)
    unweave(section_ref, dot_rows(n1_ref[...], rows).astype(BF), keep_ref, away_ref)
    acc[...] += dot_columns(rows, weave(section_ref, mine_ref, other_ref))

    @pl.when(step == 0)
    def _():
        dvec_ref[2:3, :] = column_sums(rows.astype(F32))

    @pl.when(step == 2)
    def _():
        dvec_ref[3:4, :] = column_sums(rows.astype(F32))
        dn1 = acc[...]
        unit, scale = normalized(x_ref[...].astype(F32))
        dx_ref[...] = (dx1_ref[...] + norm_back(dn1, vec_ref[0:1, :], unit, scale)).astype(BF)
        dvec_ref[0:1, :] = column_sums(dn1 * unit)
        dvec_ref[1:2, :] = column_sums(dn1)


def whole(*shape):
    return pl.BlockSpec(shape, lambda *_: (0,) * len(shape))


def stepped(*shape):
    return pl.BlockSpec(shape, lambda step: (step,) + (0,) * (len(shape) - 1))


def out(shape, kind):
    return jax.ShapeDtypeStruct(shape, kind)


def params():
    return pltpu.CompilerParams(vmem_limit_bytes=VMEM_BYTES)


def cost(us):
    return pl.CostEstimate(
        flops=int(us * 4e8), bytes_accessed=int(us * 3e6), transcendentals=0
    )


def middle(rows):
    return rows // 32 * 16


def sum_pairs_kernel(*refs):
    own_ref, low_ref, high_ref = refs[-3:]
    pairs = refs[:-3]
    on_first = lax.axis_index("group") % 2 == 0
    cut = low_ref.shape[1]
    total = [add(keep[...], got[...]).astype(BF) for keep, got in zip(pairs[::2], pairs[1::2])]
    total = jnp.concatenate(total, axis=1) if len(total) > 1 else total[0]
    own_ref[0] = lax.select(on_first, total[0], total[1])
    away = lax.select(on_first, total[1], total[0])
    low_ref[0] = away[:cut]
    high_ref[0] = away[cut:]


def sum_pairs(pairs):
    rows = sum(keep.shape[1] for keep, _ in pairs)
    cut = middle(rows)
    specs = [
        pl.BlockSpec((2, keep.shape[1], WIDTH), lambda step: (step, 0, 0))
        for keep, _ in pairs
        for _ in range(2)
    ]
    return pl.pallas_call(
        sum_pairs_kernel,
        grid=(4,),
        in_specs=specs,
        out_specs=[stepped(1, rows, WIDTH), stepped(1, cut, WIDTH), stepped(1, rows - cut, WIDTH)],
        out_shape=[
            out((4, rows, WIDTH), BF),
            out((4, cut, WIDTH), BF),
            out((4, rows - cut, WIDTH), BF),
        ],
        compiler_params=params(),
        cost_estimate=cost(5),
        name="sum_pairs",
    )(*(value for pair in pairs for value in pair))


def sum_z_kernel(own_ref, low_ref, high_ref, zero_ref, one_ref, minus_ref, two_low_ref, two_high_ref):
    x = lax.axis_index("group") // 2
    cut, half = low_ref.shape[1], two_low_ref.shape[0]

    def piece(k):
        at = lax.rem(x + k, 4)
        from_z = jnp.concatenate([low_ref[at], high_ref[at]], axis=0)
        return add(own_ref[at], from_z).astype(BF)

    zero_ref[...] = piece(0)
    one_ref[...] = piece(1)
    minus_ref[...] = piece(3)
    two = piece(2)
    two_low_ref[...] = two[:half]
    two_high_ref[...] = two[half:]


def sum_z(own, low, high):
    rows = own.shape[1]
    half = middle(rows)
    vmem = pl.BlockSpec(memory_space=pltpu.VMEM)
    return pl.pallas_call(
        sum_z_kernel,
        in_specs=[vmem] * 3,
        out_specs=[vmem] * 5,
        out_shape=[out((rows, WIDTH), BF)] * 3 + [out((half, WIDTH), BF), out((rows - half, WIDTH), BF)],
        compiler_params=params(),
        cost_estimate=cost(4),
        name="sum_z",
    )(own, low, high)


def sum_far_kernel(one_ref, minus_ref, left_ref, right_ref, one_out, minus_out):
    half = left_ref.shape[0]
    one_out[:half, :] = add(one_ref[:half, :], left_ref[...]).astype(BF)
    one_out[half:, :] = one_ref[half:, :]
    minus_out[:half, :] = minus_ref[:half, :]
    minus_out[half:, :] = add(minus_ref[half:, :], right_ref[...]).astype(BF)


def sum_far(one, minus, from_left, from_right):
    vmem = pl.BlockSpec(memory_space=pltpu.VMEM)
    return pl.pallas_call(
        sum_far_kernel,
        in_specs=[vmem] * 4,
        out_specs=[vmem] * 2,
        out_shape=[out(one.shape, BF)] * 2,
        compiler_params=params(),
        cost_estimate=cost(2),
        name="sum_far",
    )(one, minus, from_left, from_right)


SMEM_SPEC = pl.BlockSpec(memory_space=pltpu.SMEM)
HEADS_SPEC = pl.BlockSpec((GROUPS, 1, ROWS, 128), lambda step: (0, step, 0, 0))
WIDE_SPEC = pl.BlockSpec((GROUPS, HALF, WIDTH), lambda step: (0, step, 0))
OUT_SPEC = pl.BlockSpec((GROUPS, HALF, WIDTH), lambda step: (0, 3, 0))
PROJ_SPEC = pl.BlockSpec((2, 4 * HALF, WIDTH), lambda step: (step, 1, 0))
DPROJ_SPEC = pl.BlockSpec((2, 4 * HALF, WIDTH), lambda step: (step, 0, 0))


def run_pre_forward(section, x, vec, slim):
    return pl.pallas_call(
        pre_forward,
        grid=(3,),
        in_specs=[SMEM_SPEC, whole(ROWS, WIDTH), whole(12, WIDTH), WIDE_SPEC, WIDE_SPEC],
        out_specs=[whole(ROWS, WIDTH), HEADS_SPEC],
        out_shape=[out((ROWS, WIDTH), BF), out((GROUPS, 3, ROWS, 128), BF)],
        compiler_params=params(),
        cost_estimate=cost(4),
        name="pre_forward",
    )(section, x, vec, *slim)


def run_attend_forward(length_row, qkv):
    return pl.pallas_call(
        attend_forward,
        grid=(1,),
        in_specs=[SMEM_SPEC, whole(GROUPS, 3, ROWS, 128)],
        out_specs=[whole(GROUPS, ROWS, 128), whole(SEQ, 128)],
        out_shape=[out((GROUPS, ROWS, 128), BF), out((SEQ, 128), F32)],
        compiler_params=params(),
        cost_estimate=cost(8),
        name="attend_forward",
    )(length_row, qkv)


def run_attend_backward(length_row, qkv, grad, logsum):
    return pl.pallas_call(
        attend_backward,
        grid=(1,),
        in_specs=[
            SMEM_SPEC,
            whole(GROUPS, 3, ROWS, 128),
            whole(GROUPS, ROWS, 128),
            whole(SEQ, 128),
        ],
        out_specs=whole(GROUPS, 3, ROWS, 128),
        out_shape=out((GROUPS, 3, ROWS, 128), BF),
        scratch_shapes=[pltpu.VMEM((SEQ, 128), F32), pltpu.VMEM((SEQ, 128), F32)],
        compiler_params=params(),
        cost_estimate=cost(16),
        name="attend_backward",
    )(length_row, qkv, grad, logsum)


def run_post_forward(section, mixed, x, vec, slim, wide):
    return pl.pallas_call(
        post_forward,
        grid=(4,),
        in_specs=[
            SMEM_SPEC,
            whole(GROUPS, ROWS, 128),
            whole(ROWS, WIDTH),
            whole(12, WIDTH),
            OUT_SPEC,
            OUT_SPEC,
            WIDE_SPEC,
            WIDE_SPEC,
            PROJ_SPEC,
            PROJ_SPEC,
        ],
        out_specs=[
            whole(ROWS, WIDTH),
            whole(ROWS, WIDTH),
            whole(ROWS, WIDTH),
            stepped(1, ROWS, WIDTH),
        ],
        out_shape=[
            out((ROWS, WIDTH), BF),
            out((ROWS, WIDTH), F32),
            out((ROWS, WIDTH), BF),
            out((4, ROWS, WIDTH), F32),
        ],
        scratch_shapes=[pltpu.VMEM((ROWS, WIDTH), F32)],
        compiler_params=params(),
        cost_estimate=cost(8),
        name="post_forward",
    )(section, mixed, x, vec, *slim, *wide, *wide)


def run_post_backward(section, dy, u, n2, x1, mixed, vec, slim, wide):
    return pl.pallas_call(
        post_backward,
        grid=(4,),
        in_specs=[
            SMEM_SPEC,
            whole(ROWS, WIDTH),
            stepped(1, ROWS, WIDTH),
            whole(ROWS, WIDTH),
            whole(ROWS, WIDTH),
            whole(GROUPS, ROWS, 128),
            whole(12, WIDTH),
            OUT_SPEC,
            OUT_SPEC,
            WIDE_SPEC,
            WIDE_SPEC,
            PROJ_SPEC,
            PROJ_SPEC,
        ],
        out_specs=[
            whole(ROWS, WIDTH),
            whole(GROUPS, ROWS, 128),
            whole(12, WIDTH),
            whole(GROUPS, HALF, WIDTH),
            whole(GROUPS, HALF, WIDTH),
            WIDE_SPEC,
            WIDE_SPEC,
            DPROJ_SPEC,
            DPROJ_SPEC,
        ],
        out_shape=[
            out((ROWS, WIDTH), F32),
            out((GROUPS, ROWS, 128), BF),
            out((12, WIDTH), F32),
            out((GROUPS, HALF, WIDTH), BF),
            out((GROUPS, HALF, WIDTH), BF),
            out((GROUPS, 4 * HALF, WIDTH), BF),
            out((GROUPS, 4 * HALF, WIDTH), BF),
            out((GROUPS, 4 * HALF, WIDTH), BF),
            out((GROUPS, 4 * HALF, WIDTH), BF),
        ],
        scratch_shapes=[pltpu.VMEM((ROWS, WIDTH), F32)],
        compiler_params=params(),
        cost_estimate=cost(14),
        name="post_backward",
    )(section, dy, u, n2, x1, mixed, vec, *slim, *wide, *wide)


def run_pre_backward(section, grads, n1, x, dx1, vec, slim):
    return pl.pallas_call(
        pre_backward,
        grid=(3,),
        in_specs=[
            SMEM_SPEC,
            HEADS_SPEC,
            whole(ROWS, WIDTH),
            whole(ROWS, WIDTH),
            whole(ROWS, WIDTH),
            whole(12, WIDTH),
            WIDE_SPEC,
            WIDE_SPEC,
        ],
        out_specs=[whole(ROWS, WIDTH), whole(12, WIDTH), WIDE_SPEC, WIDE_SPEC],
        out_shape=[
            out((ROWS, WIDTH), BF),
            out((12, WIDTH), F32),
            out((GROUPS, 3 * HALF, WIDTH), BF),
            out((GROUPS, 3 * HALF, WIDTH), BF),
        ],
        scratch_shapes=[pltpu.VMEM((ROWS, WIDTH), F32)],
        compiler_params=params(),
        cost_estimate=cost(8),
        name="pre_backward",
    )(section, grads, n1, x, dx1, vec, *slim)


def exchange(value):
    return lax.all_to_all(value, "group", 0, 0, tiled=True)


def body(
    tokens,
    cotangent,
    lengths,
    ln1_gain,
    ln1_bias,
    w_qkv,
    b_query,
    b_value,
    w_out,
    b_out,
    ln2_gain,
    ln2_bias,
    w_fc,
    b_fc,
    w_proj,
    b_proj,
):
    section = lax.axis_index("section")
    which = section.astype(jnp.int32).reshape(1)
    length_row = lax.dynamic_index_in_dim(lengths, section, 0, keepdims=False)
    tokens_row = lax.dynamic_index_in_dim(tokens, section, 0, keepdims=False)

    vectors = (ln1_gain, ln1_bias, b_query, b_value, b_out, ln2_gain, ln2_bias, b_proj)
    keep, away = run_pack_shard(which, w_qkv, w_out, w_fc, w_proj, b_fc, *vectors)
    got = swap(away)
    shard_zero, shard_one = pick(keep, got), pick(got, keep)
    front = SLIM + VEC_ROWS
    slim_zero = Gather(jnp.concatenate([shard_zero[:front], shard_one[SLIM:front]], axis=0))
    wide_zero = Gather(shard_zero[front:])
    slim_one = Gather(shard_one[:SLIM])
    wide_one = Gather(shard_one[front:])

    slim_zero.near()
    wide_zero.shard = slim_zero.after(wide_zero.shard)
    slim_zero.far()
    wide_zero.shard = slim_zero.after(wide_zero.shard)
    slim_zero.last()
    wide_zero.near()
    mine = slim_zero.whole()
    slim = mine, swap(mine)
    vecs = run_unpack_vectors(mine)

    n1, send = run_pre_forward(which, tokens_row, vecs[0], slim)
    send = wide_zero.after(send)
    wide_zero.far()
    heads = exchange(send)
    heads = wide_zero.after(heads)
    slim_one.shard, heads = tie(slim_one.shard, heads)
    wide_zero.last()
    slim_one.near()
    mixed, logsum = run_attend_forward(length_row, heads)
    mixed = wide_zero.after(mixed)
    mine = wide_zero.whole()
    wide = mine, swap(mine)
    mixed = exchange(mixed)
    mixed = slim_one.after(mixed)
    wide_one.shard, mixed = tie(wide_one.shard, mixed)
    slim_one.far()
    result, x1, n2, u = run_post_forward(which, mixed, tokens_row, vecs[0], slim, wide)
    kept_zero = (tokens_row, n1, heads, logsum, mixed, x1, n2, u, slim, wide)

    result = slim_one.after(result)
    wide_one.shard, result = tie(wide_one.shard, result)
    output_zero = result
    slim_one.last()
    wide_one.near()
    mine = slim_one.whole()
    slim = mine, swap(mine)
    n1, send = run_pre_forward(which, result, vecs[1], slim)
    send = wide_one.after(send)
    wide_one.far()
    heads = exchange(send)
    heads = wide_one.after(heads)
    wide_one.last()
    mixed, logsum = run_attend_forward(length_row, heads)
    mixed = wide_one.after(mixed)
    mine = wide_one.whole()
    wide = mine, swap(mine)
    mixed = exchange(mixed)
    output_one, x1, n2, u = run_post_forward(which, mixed, result, vecs[1], slim, wide)
    kept_one = (result, n1, heads, logsum, mixed, x1, n2, u, slim, wide)

    def first_part(layer, grad, kept):
        _, _, _, _, mixed, x1, n2, u, slim, wide = kept
        dx1, send, dvec, *halves = run_post_backward(
            which, grad, u, n2, x1, mixed, vecs[layer], slim, wide
        )
        pairs = [(keep, swap(away)) for keep, away in zip(halves[::2], halves[1::2])]
        return dx1, send, dvec, pairs

    def second_part(layer, dheads, dx1, kept):
        rows, n1, _, _, _, _, _, _, slim, _ = kept
        grad, dvec, keep, away = run_pre_backward(which, dheads, n1, rows, dx1, vecs[layer], slim)
        return grad, dvec, (keep, swap(away))

    grad = lax.dynamic_index_in_dim(cotangent, section, 0, keepdims=False)
    dx1, send, dvec_two, pairs = first_part(1, grad, kept_one)
    bulk_one = GroupSum(pairs)
    dheads = run_attend_backward(length_row, kept_one[2], exchange(send), kept_one[3])
    dheads = exchange(dheads)
    bulk_one.low, bulk_one.high, dheads = tie(bulk_one.low, bulk_one.high, dheads)
    bulk_one.far()
    grad_one, dvec_one, slim_pair = second_part(1, dheads, dx1, kept_one)
    dvec_last = dvec_one + dvec_two

    dx1, send, dvec_two, pairs = first_part(0, grad_one, kept_zero)
    bulk_one.from_left, bulk_one.from_right, send = tie(
        bulk_one.from_left, bulk_one.from_right, send
    )
    bulk = GroupSum([*pairs, slim_pair])
    grad_heads = exchange(send)
    bulk_one.from_left, bulk_one.from_right, grad_heads = tie(
        bulk_one.from_left, bulk_one.from_right, grad_heads
    )
    bulk_one.near()
    dheads = run_attend_backward(length_row, kept_zero[2], grad_heads, kept_zero[3])
    dheads = exchange(dheads)
    bulk.low, bulk.high, bulk_one.one, bulk_one.minus, dheads = tie(
        bulk.low, bulk.high, bulk_one.one, bulk_one.minus, dheads
    )
    bulk.far()
    grad_zero, dvec_one, slim_pair = second_part(0, dheads, dx1, kept_zero)
    dvecs = jnp.stack([dvec_one + dvec_two, dvec_last])
    dvecs = dvecs + swap(dvecs)
    slim_sum = add(*slim_pair).astype(BF)
    last = jnp.concatenate([slim_sum, run_pack_vectors(dvecs)], axis=1)
    last, bulk.from_left, bulk.from_right = tie(last, bulk.from_left, bulk.from_right)
    bulk.near()
    last = over_all(last)
    split = HALF + WIDE
    both = jnp.concatenate([bulk.total(), bulk_one.total()], axis=0)
    both = over_replica(both)
    bulk, sum_one = both[: split + 3 * HALF], both[split + 3 * HALF :]

    def own_layer(zero, one):
        mine, other = pick(zero, one), swap(pick(one, zero))
        return pick(mine, other).astype(F32), pick(other, mine).astype(F32)

    first, second = own_layer(bulk[:split], sum_one)
    first_slim, second_slim = own_layer(last[: 3 * HALF], bulk[split:])

    def block(low, high, j):
        at = slice(HALF * j, HALF * j + HALF)
        return jnp.concatenate([low[at], high[at]], axis=0)

    grad_qkv = jnp.concatenate([block(first_slim, second_slim, j) for j in range(3)], axis=1)
    grad_out = block(first, second, 0)
    grad_fc = jnp.concatenate([block(first, second, 1 + j) for j in range(4)], axis=1)
    grad_proj = jnp.concatenate([first[5 * HALF :], second[5 * HALF :]], axis=0)
    v = last[3 * HALF :].astype(F32)
    v = pick(v[:VEC_ROWS], v[VEC_ROWS:])

    def both_micro(zero, one):
        mine, other = pick(zero, one), swap(pick(one, zero))
        return jnp.stack([pick(mine, other), pick(other, mine)])[None]

    acts = both_micro(output_zero, output_one)
    in_grads = both_micro(grad_zero, grad_one)
    return (
        acts,
        in_grads,
        v[0:1, :SHARD],
        v[1:2, :SHARD],
        grad_qkv[None],
        v[2:3, :SHARD],
        v[3:4, :SHARD],
        grad_out[None],
        v[4:5, :SHARD],
        v[5:6, :SHARD],
        v[6:7, :SHARD],
        grad_fc[None],
        v[8:9, : 4 * SHARD],
        grad_proj[None],
        v[7:8, :SHARD],
    )


def solution(mesh):
    placed = (
        P("replica", "group", None),
        P("replica", "group", None),
        P("replica", None),
        P("section", "group"),
        P("section", "group"),
        P("section", "group", None),
        P("section", "group"),
        P("section", "group"),
        P("section", "group", None),
        P("section", "group"),
        P("section", "group"),
        P("section", "group"),
        P("section", "group", None),
        P("section", "group"),
        P("section", "group", None),
        P("section", "group"),
    )
    return jax.shard_map(
        body,
        mesh=mesh,
        in_specs=placed,
        out_specs=(
            P("section", "replica", "group", None),
            P("section", "replica", "group", None),
            P("section", "group"),
            P("section", "group"),
            P("section", "group", None),
            P("section", "group"),
            P("section", "group"),
            P("section", "group", None),
            P("section", "group"),
            P("section", "group"),
            P("section", "group"),
            P("section", "group", None),
            P("section", "group"),
            P("section", "group", None),
            P("section", "group"),
        ),
        check_vma=False,
    )
```

```python
import functools

import jax
import jax.numpy as jnp
from jax import lax
from jax.experimental import pallas as pl
from jax.experimental.pallas import tpu as pltpu
from jax.sharding import PartitionSpec as P

WIDTH = 768
GROUPS = 8
PAIRS = 6
SEQ = 1024
ROWS = 128
BLOCK = 256
SHARD = 96
HALF = 48
SLIM = 192
WIDE = 384
VEC_ROWS = 16
EPSILON = 1e-05
VMEM_BYTES = 40 * 1024 * 1024
GELU_C = 0.7978845608028654
BF = jnp.bfloat16
F32 = jnp.float32


def torus_pairs(move):
    pairs = []
    for source in range(64):
        group, replica = divmod(source, 8)
        x, z_lo = divmod(group, 2)
        z_hi, y = divmod(replica, 4)
        x, y, z = move(x, y, z_hi * 2 + z_lo)
        pairs.append((source, ((x % 4) * 2 + z % 2) * 8 + (z % 4) // 2 * 4 + y % 4))
    return pairs


def along_x(value, by):
    return lax.ppermute(value, ("group", "replica"), torus_pairs(lambda x, y, z: (x + by, y, z)))


def along_y(value, by):
    return lax.ppermute(value, ("group", "replica"), torus_pairs(lambda x, y, z: (x, y + by, z)))


def along_z(value, by):
    return lax.ppermute(value, ("group", "replica"), torus_pairs(lambda x, y, z: (x, y, z + by)))


def swap(value):
    return lax.ppermute(value, "section", [(0, 1), (1, 0)])


def tie(*values):
    return lax.optimization_barrier(values)


def pick(on_first, on_second):
    return jnp.where(lax.axis_index("section") == 0, on_first, on_second)


def after(holder, names, value):
    tied = tie(*(getattr(holder, name) for name in names), value)
    for name, part in zip(names, tied):
        setattr(holder, name, part)
    return tied[-1]


class Gather:
    def __init__(self, shard):
        self.shard = shard
        self.cut = shard.shape[0] // 2

    def near(self):
        shard, cut = self.shard, self.cut
        self.left = along_x(shard, 1)
        self.right = along_x(shard, -1)
        self.z_low = along_z(shard[:cut], 1)
        self.z_high = along_z(shard[cut:], -1)

    def far(self):
        cut = self.cut
        self.far_low = along_x(self.left[:cut], 1)
        self.far_high = along_x(self.right[cut:], -1)
        self.z_left = along_z(self.left, 1)
        self.z_right = along_z(self.right, -1)

    def last(self):
        self.z_far_low = along_z(self.far_low, 1)
        self.z_far_high = along_z(self.far_high, -1)

    def after(self, *values):
        names = [name for name in vars(self) if name not in ("cut",)]
        count = len(names)
        tied = tie(*(getattr(self, name) for name in names), *values)
        for name, value in zip(names, tied):
            setattr(self, name, value)
        return tied[count:] if len(values) != 1 else tied[count]

    def whole(self):
        pieces = (
            self.shard,
            self.left,
            self.right,
            self.far_low,
            self.far_high,
            self.z_low,
            self.z_high,
            self.z_left,
            self.z_right,
            self.z_far_low,
            self.z_far_high,
        )
        return assemble(self.cut, *pieces)


def add(left, right):
    return left.astype(F32) + right.astype(F32)


class GroupSum:
    def __init__(self, pairs):
        self.own, away_low, away_high = sum_pairs_z(pairs)
        self.low = along_z(away_low, 1)
        self.high = along_z(away_high, -1)

    def far(self):
        self.zero, self.one, self.minus, two_low, two_high = sum_z(self.own, self.low, self.high)
        self.from_left = along_x(two_low, 1)
        self.from_right = along_x(two_high, -1)

    def near(self):
        one, minus = sum_far(self.one, self.minus, self.from_left, self.from_right)
        self.one = along_x(one, 1)
        self.minus = along_x(minus, -1)

    def total(self):
        return self.zero.astype(F32) + self.one.astype(F32) + self.minus.astype(F32)


class RingSum:
    def __init__(self, parts, place, along):
        self.parts, self.place, self.along = parts, place, along
        self.cut = parts.shape[1] // 2

    def piece(self, k):
        return lax.dynamic_index_in_dim(self.parts, lax.rem(self.place + k, 4), 0, keepdims=False)

    def far(self):
        two, cut = self.piece(2), self.cut
        self.from_left = self.along(two[:cut], 1)
        self.from_right = self.along(two[cut:], -1)

    def near(self):
        one, minus, cut = self.piece(1), self.piece(3), self.cut
        one = jnp.concatenate([add(one[:cut], self.from_left).astype(BF), one[cut:]], axis=0)
        minus = jnp.concatenate([minus[:cut], add(minus[cut:], self.from_right).astype(BF)], axis=0)
        self.one = self.along(one, 1)
        self.minus = self.along(minus, -1)

    def total(self):
        return self.piece(0).astype(F32) + self.one.astype(F32) + self.minus.astype(F32)


class BulkSum:
    def __init__(self, pairs):
        self.zero, self.one, self.minus, self.two_low, self.two_high = sum_pairs(pairs)

    def y_far(self):
        self.from_left = along_y(self.two_low, 1)
        self.from_right = along_y(self.two_high, -1)

    def y_near(self):
        one, minus = sum_far(self.one, self.minus, self.from_left, self.from_right)
        self.one = along_y(one, 1)
        self.minus = along_y(minus, -1)

    def over_z(self):
        self.own, low, high = sum_y(self.zero, self.one, self.minus)
        self.low = along_z(low, 1)
        self.high = along_z(high, -1)

    def x_far(self):
        self.zero, self.one, self.minus, two_low, two_high = sum_z(self.own, self.low, self.high)
        self.from_left = along_x(two_low, 1)
        self.from_right = along_x(two_high, -1)

    def x_near(self):
        one, minus = sum_far(self.one, self.minus, self.from_left, self.from_right)
        self.one = along_x(one, 1)
        self.minus = along_x(minus, -1)

    def total(self):
        return self.zero.astype(F32) + self.one.astype(F32) + self.minus.astype(F32)

def every_part(total, whole):
    z_hi, y = jnp.divmod(lax.axis_index("replica"), 4)
    rows, piece = total.shape[0], whole.shape[0]
    mine = jnp.concatenate([total.astype(BF), whole], axis=0)
    other = along_z(mine, 2)
    both = add(mine[:rows], other[:rows]).astype(BF)
    first, second = mine[rows:], other[rows:]
    first, second = jnp.where(z_hi == 0, first, second), jnp.where(z_hi == 0, second, first)
    mine = jnp.concatenate([both, first, second], axis=0)
    half = mine.shape[0] // 2
    left = along_y(mine, 1)
    right = along_y(mine, -1)
    far = jnp.concatenate([along_y(left[:half], 1), along_y(right[half:], -1)], axis=0)
    full = jnp.zeros((4,) + mine.shape, BF)
    for part, k in ((mine, 0), (left, 3), (right, 1), (far, 2)):
        full = lax.dynamic_update_slice(full, part[None], (lax.rem(y + k, 4), 0, 0))
    last = full[:, rows:].reshape(4, 2, piece, WIDTH).transpose(1, 0, 2, 3)
    return full[:, :rows], last.reshape(-1, WIDTH)


def dot(left, right):
    return jnp.dot(left, right, preferred_element_type=F32)


def dot_rows(left, right):
    return lax.dot_general(left, right, (((0,), (0,)), ((), ())), preferred_element_type=F32)


def dot_columns(left, right):
    return lax.dot_general(left, right, (((1,), (1,)), ((), ())), preferred_element_type=F32)


def normalized(rows):
    center = rows - jnp.mean(rows, axis=-1, keepdims=True)
    scale = lax.rsqrt(jnp.mean(center * center, axis=-1, keepdims=True) + EPSILON)
    return center * scale, scale


def norm_back(grad, gain, unit, scale):
    inner = grad * gain
    return scale * (
        inner
        - jnp.mean(inner, axis=-1, keepdims=True)
        - unit * jnp.mean(inner * unit, axis=-1, keepdims=True)
    )


def column_sums(rows):
    return jnp.sum(rows, axis=0, keepdims=True)


PLACES = (
    (0, False, False),
    (3, False, False),
    (1, False, False),
    (2, False, False),
    (2, False, True),
    (0, True, False),
    (0, True, True),
    (3, True, False),
    (1, True, False),
    (2, True, False),
    (2, True, True),
)


def assemble_rows(cut, *refs):
    pieces, full = refs[: len(PLACES)], refs[len(PLACES)]
    group = lax.axis_index("group")
    x, z = group // 2, group % 2
    for piece, (dx, flip, high) in zip(pieces, PLACES):
        at = lax.rem(x + dx, 4) * 2 + (1 - z if flip else z)
        row = cut if high else 0
        full[pl.ds(at, 1), row : row + piece.shape[0]] = piece[...][None]


def assemble(cut, *pieces):
    rows = pieces[0].shape[0]
    return pl.pallas_call(
        functools.partial(assemble_rows, cut),
        in_specs=[pl.BlockSpec(memory_space=pltpu.VMEM)] * len(PLACES),
        out_specs=pl.BlockSpec(memory_space=pltpu.VMEM),
        out_shape=jax.ShapeDtypeStruct((GROUPS, rows, WIDTH), BF),
        compiler_params=pltpu.CompilerParams(vmem_limit_bytes=VMEM_BYTES),
        cost_estimate=cost(4),
        name="assemble",
    )(*pieces)


def pack_shard(section_ref, qkv_ref, out_ref, fc_ref, proj_ref, bias_ref, *refs):
    vectors, (keep_ref, away_ref) = refs[:8], refs[8:]
    on_first = section_ref[0] == 0

    def put(row, low, high):
        at = slice(row, row + low.shape[0])
        keep_ref[at, :] = lax.select(on_first, low, high)
        away_ref[at, :] = lax.select(on_first, high, low)

    for j in range(3):
        at = slice(WIDTH * j, WIDTH * (j + 1))
        put(HALF * j, qkv_ref[0, :HALF, at], qkv_ref[0, HALF:, at])
    put(3 * HALF, out_ref[0, :HALF], out_ref[0, HALF:])
    for j in range(4):
        at = slice(WIDTH * j, WIDTH * (j + 1))
        put(SLIM + VEC_ROWS + HALF * j, fc_ref[0, :HALF, at], fc_ref[0, HALF:, at])
    put(SLIM + VEC_ROWS + 4 * HALF, proj_ref[0, : 4 * HALF], proj_ref[0, 4 * HALF :])
    rows = jnp.concatenate([ref[...].astype(F32) for ref in vectors], axis=0)
    rows = jnp.concatenate([rows, jnp.zeros((8, WIDTH - SHARD), F32)], axis=1)
    bias = jnp.concatenate([bias_ref[...].astype(F32), jnp.zeros((1, WIDTH // 2), F32)], axis=1)
    rows = jnp.concatenate([rows, bias, jnp.zeros((7, WIDTH), F32)], axis=0).astype(BF)
    put(SLIM, rows, rows)


def run_pack_shard(section, qkv, out_w, fc, proj, bias, *vectors):
    shape = jax.ShapeDtypeStruct((SLIM + VEC_ROWS + WIDE, WIDTH), BF)
    return pl.pallas_call(
        pack_shard,
        grid=(1,),
        in_specs=[pl.BlockSpec(memory_space=pltpu.SMEM)]
        + [whole(*value.shape) for value in (qkv, out_w, fc, proj, bias, *vectors)],
        out_specs=[whole(*shape.shape)] * 2,
        out_shape=[shape, shape],
        compiler_params=pltpu.CompilerParams(vmem_limit_bytes=VMEM_BYTES),
        cost_estimate=cost(3),
        name="pack_shard",
    )(section, qkv, out_w, fc, proj, bias, *vectors)


def one_hot(group):
    row = lax.broadcasted_iota(jnp.int32, (128, WIDTH), 0)
    lane = lax.broadcasted_iota(jnp.int32, (128, WIDTH), 1)
    return jnp.where((lane == row + SHARD * group) & (row < SHARD), 1.0, 0.0).astype(BF)


def unpack_vectors(mine_ref, vecs_ref):
    total = jnp.zeros((2 * VEC_ROWS, WIDTH), F32)
    for group in range(GROUPS):
        total = total + dot(mine_ref[group, :, :128], one_hot(group))
    for layer in range(2):
        vecs_ref[layer, 0:8, :] = total[VEC_ROWS * layer : VEC_ROWS * layer + 8]
        for j in range(4):
            for side in range(2):
                piece = mine_ref[2 * j + side, VEC_ROWS * layer : VEC_ROWS * (layer + 1), : WIDTH // 2]
                at = slice(side * (WIDTH // 2), (side + 1) * (WIDTH // 2))
                vecs_ref[layer, 8 + j : 9 + j, at] = piece.astype(F32)[8:9]


def run_unpack_vectors(mine):
    return pl.pallas_call(
        unpack_vectors,
        grid=(1,),
        in_specs=[pl.BlockSpec((GROUPS, 2 * VEC_ROWS, WIDTH), lambda step: (0, SLIM // (2 * VEC_ROWS), 0))],
        out_specs=whole(2, 12, WIDTH),
        out_shape=jax.ShapeDtypeStruct((2, 12, WIDTH), F32),
        cost_estimate=cost(2),
        name="unpack_vectors",
    )(mine)


def pack_last(keep_ref, got_ref, vecs_ref, other_vecs_ref, out_ref):
    rows = keep_ref.shape[1]
    for group in range(GROUPS):
        out_ref[group, :rows] = add(keep_ref[group], got_ref[group]).astype(BF)
        for layer in range(2):
            plain = vecs_ref[layer, 0:8, :] + other_vecs_ref[layer, 0:8, :]
            plain = lax.dot_general(
                plain.astype(BF), one_hot(group), (((1,), (1,)), ((), ())), preferred_element_type=F32
            )
            plain = jnp.concatenate([plain, jnp.zeros((8, WIDTH - 128), F32)], axis=1)
            side = group % 2
            at = slice(side * (WIDTH // 2), (side + 1) * (WIDTH // 2))
            row = slice(8 + group // 2, 9 + group // 2)
            bias = vecs_ref[layer, row, at] + other_vecs_ref[layer, row, at]
            bias = jnp.concatenate([bias, jnp.zeros((1, WIDTH // 2), F32)], axis=1)
            plain = jnp.concatenate([plain, bias, jnp.zeros((7, WIDTH), F32)], axis=0)
            low = rows + VEC_ROWS * layer
            out_ref[group, low : low + VEC_ROWS] = plain.astype(BF)


def run_pack_last(keep, got, vecs, other_vecs):
    vmem = pl.BlockSpec(memory_space=pltpu.VMEM)
    rows = keep.shape[1] + 2 * VEC_ROWS
    return pl.pallas_call(
        pack_last,
        in_specs=[vmem] * 4,
        out_specs=vmem,
        out_shape=jax.ShapeDtypeStruct((GROUPS, rows, WIDTH), BF),
        compiler_params=pltpu.CompilerParams(vmem_limit_bytes=VMEM_BYTES),
        cost_estimate=cost(3),
        name="pack_last",
    )(keep, got, vecs, other_vecs)


def put_pairs(ref, rows, *index):
    for pair in range(PAIRS):
        ref[(pair, *index)] = rows[:, pair * 128 : (pair + 1) * 128]
    for pair in range(PAIRS, GROUPS):
        ref[(pair, *index)] = jnp.zeros((ROWS, 128), BF)


def weave(section_ref, mine_ref, other_ref):
    on_first = section_ref[0] == 0
    mine, other = mine_ref[...], other_ref[...]
    both = [lax.select(on_first, mine, other), lax.select(on_first, other, mine)]
    return jnp.concatenate(both, axis=1).reshape(WIDTH, WIDTH)


def unweave(section_ref, rows, keep_ref, away_ref):
    on_first = section_ref[0] == 0
    groups, half, _ = keep_ref.shape
    rows = rows.reshape(groups, 2 * half, WIDTH)
    low, high = rows[:, :half], rows[:, half:]
    keep_ref[...] = lax.select(on_first, low, high)
    away_ref[...] = lax.select(on_first, high, low)


def pre_forward(section_ref, x_ref, vec_ref, mine_ref, other_ref, n1_ref, send_ref):
    step = pl.program_id(0)

    @pl.when(step == 0)
    def _():
        unit, _ = normalized(x_ref[...].astype(F32))
        n1_ref[...] = (unit * vec_ref[0:1, :] + vec_ref[1:2, :]).astype(BF)

    bias = jnp.where(step == 0, vec_ref[2:3, :], jnp.where(step == 2, vec_ref[3:4, :], 0.0))
    product = dot(n1_ref[...], weave(section_ref, mine_ref, other_ref))
    put_pairs(send_ref, (product + bias).astype(BF), 0)


def visible(length_ref, at, columns):
    first_end = length_ref[0]
    second_end = first_end + length_ref[1]
    row = lax.broadcasted_iota(jnp.int32, (BLOCK, 1), 0) + at
    start = jnp.where(row >= second_end, second_end, jnp.where(row >= first_end, first_end, 0))
    column = lax.broadcasted_iota(jnp.int32, (BLOCK, columns), 1)
    return (column >= start) & (column <= row)


def of_head(rows, head):
    lane = lax.broadcasted_iota(jnp.int32, rows.shape, 1)
    keep = lane < 64 if head == 0 else lane >= 64
    return jnp.where(keep, rows, jnp.zeros_like(rows))


def both_heads(first, second):
    lane = lax.broadcasted_iota(jnp.int32, first.shape, 1)
    return jnp.where(lane < 64, first, second)


def attend_forward(length_ref, qkv_ref, out_ref, logsum_ref):
    for block in range(SEQ // BLOCK):
        keys = (block + 1) * BLOCK
        query = qkv_ref[2 * block : 2 * block + 2, 0].reshape(BLOCK, 128)
        query = (query.astype(F32) * 0.125).astype(BF)
        key = qkv_ref[: 2 * block + 2, 1].reshape(keys, 128)
        value = qkv_ref[: 2 * block + 2, 2].reshape(keys, 128)
        allowed = visible(length_ref, block * BLOCK, keys)
        mixed, sums = [], []
        for head in range(2):
            scores = dot_columns(of_head(query, head), key)
            scores = jnp.where(allowed, scores, -1e30)
            maximum = jnp.max(scores, axis=-1, keepdims=True)
            expo = jnp.exp(scores - maximum)
            total = jnp.sum(expo, axis=-1, keepdims=True)
            mixed.append(dot((expo * (1.0 / total)).astype(BF), value))
            sums.append(jnp.broadcast_to(maximum + jnp.log(total), (BLOCK, 128)))
        out_ref[2 * block : 2 * block + 2] = both_heads(*mixed).astype(BF).reshape(2, 128, 128)
        logsum_ref[block * BLOCK : (block + 1) * BLOCK, :] = both_heads(*sums)


def attend_backward(length_ref, qkv_ref, grad_ref, logsum_ref, out_ref, key_acc, value_acc):
    key_acc[...] = jnp.zeros_like(key_acc)
    value_acc[...] = jnp.zeros_like(value_acc)
    for block in range(SEQ // BLOCK):
        keys = (block + 1) * BLOCK
        query = qkv_ref[2 * block : 2 * block + 2, 0].reshape(BLOCK, 128)
        query = (query.astype(F32) * 0.125).astype(BF)
        grad = grad_ref[2 * block : 2 * block + 2].reshape(BLOCK, 128)
        key = qkv_ref[: 2 * block + 2, 1].reshape(keys, 128)
        value = qkv_ref[: 2 * block + 2, 2].reshape(keys, 128)
        allowed = visible(length_ref, block * BLOCK, keys)
        grad_query = []
        for head in range(2):
            query_one, grad_one = of_head(query, head), of_head(grad, head)
            logsum = logsum_ref[block * BLOCK : (block + 1) * BLOCK, 64 * head : 64 * head + 1]
            scores = jnp.where(allowed, dot_columns(query_one, key), -1e30)
            probs = jnp.exp(scores - logsum)
            grad_probs = dot_columns(grad_one, value)
            delta = jnp.sum(probs * grad_probs, axis=-1, keepdims=True)
            grad_scores = (probs * (grad_probs - delta)).astype(BF)
            grad_query.append(dot(grad_scores, key))
            key_acc[:keys, :] += dot_rows(grad_scores, query_one)
            value_acc[:keys, :] += dot_rows(probs.astype(BF), grad_one)
        out = (both_heads(*grad_query) * 0.125).astype(BF)
        out_ref[2 * block : 2 * block + 2, 0] = out.reshape(2, 128, 128)
    out_ref[:, 1] = key_acc[...].astype(BF).reshape(GROUPS, 128, 128)
    out_ref[:, 2] = value_acc[...].astype(BF).reshape(GROUPS, 128, 128)


def post_forward(
    section_ref,
    mixed_ref,
    x_ref,
    vec_ref,
    out_mine,
    out_other,
    fc_mine,
    fc_other,
    proj_mine,
    proj_other,
    y_ref,
    x1_ref,
    n2_ref,
    u_ref,
    acc,
):
    step = pl.program_id(0)

    @pl.when(step == 0)
    def _():
        mixed = jnp.concatenate([mixed_ref[pair] for pair in range(PAIRS)], axis=1)
        x1 = x_ref[...].astype(F32) + dot(mixed, weave(section_ref, out_mine, out_other))
        x1 = x1 + vec_ref[4:5, :]
        x1_ref[...] = x1
        unit, _ = normalized(x1)
        n2_ref[...] = (unit * vec_ref[5:6, :] + vec_ref[6:7, :]).astype(BF)
        acc[...] = x1 + vec_ref[7:8, :]

    u = dot(n2_ref[...], weave(section_ref, fc_mine, fc_other)) + vec_ref[pl.ds(8 + step, 1), :]
    u_ref[0] = u
    active = 0.5 * u * (1.0 + jnp.tanh(GELU_C * (u + 0.044715 * (u * u * u))))
    acc[...] += dot(active.astype(BF), weave(section_ref, proj_mine, proj_other))

    @pl.when(step == 3)
    def _():
        y_ref[...] = acc[...].astype(BF)


def post_backward(
    section_ref,
    dy_ref,
    u_ref,
    n2_ref,
    x1_ref,
    mixed_ref,
    vec_ref,
    out_mine,
    out_other,
    fc_mine,
    fc_other,
    proj_mine,
    proj_other,
    dx1_ref,
    send_ref,
    dvec_ref,
    dout_keep,
    dout_away,
    dfc_keep,
    dfc_away,
    dproj_keep,
    dproj_away,
    acc,
):
    step = pl.program_id(0)
    dy = dy_ref[...].astype(F32)
    low = dy.astype(BF)

    @pl.when(step == 0)
    def _():
        acc[...] = jnp.zeros_like(acc)

    u = u_ref[0]
    square = u * u
    tanh = jnp.tanh(GELU_C * (u + 0.044715 * (square * u)))
    active = (0.5 * u * (1.0 + tanh)).astype(BF)
    slope = 0.5 * (1.0 + tanh) + 0.5 * u * (1.0 - tanh * tanh) * (
        GELU_C * (1.0 + 3.0 * 0.044715 * square)
    )
    du = (dot_columns(low, weave(section_ref, proj_mine, proj_other)) * slope).astype(BF)
    unweave(section_ref, dot_rows(active, low).astype(BF), dproj_keep, dproj_away)
    unweave(section_ref, dot_rows(n2_ref[...], du).astype(BF), dfc_keep, dfc_away)
    dvec_ref[pl.ds(8 + step, 1), :] = column_sums(du.astype(F32))
    acc[...] += dot_columns(du, weave(section_ref, fc_mine, fc_other))

    @pl.when(step == 3)
    def _():
        dn2 = acc[...]
        unit, scale = normalized(x1_ref[...])
        dx1 = dy + norm_back(dn2, vec_ref[5:6, :], unit, scale)
        dx1_ref[...] = dx1
        back = dx1.astype(BF)
        mixed = jnp.concatenate([mixed_ref[pair] for pair in range(PAIRS)], axis=1)
        unweave(section_ref, dot_rows(mixed, back).astype(BF), dout_keep, dout_away)
        put_pairs(send_ref, dot_columns(back, weave(section_ref, out_mine, out_other)).astype(BF))
        dvec_ref[0:4, :] = jnp.zeros((4, WIDTH), F32)
        dvec_ref[4:5, :] = column_sums(back.astype(F32))
        dvec_ref[5:6, :] = column_sums(dn2 * unit)
        dvec_ref[6:7, :] = column_sums(dn2)
        dvec_ref[7:8, :] = column_sums(low.astype(F32))


def pre_backward(
    section_ref,
    grads_ref,
    n1_ref,
    x_ref,
    dx1_ref,
    vec_ref,
    mine_ref,
    other_ref,
    dx_ref,
    dvec_ref,
    keep_ref,
    away_ref,
    acc,
):
    step = pl.program_id(0)

    @pl.when(step == 0)
    def _():
        acc[...] = jnp.zeros_like(acc)
        dvec_ref[...] = jnp.zeros_like(dvec_ref)

    rows = jnp.concatenate([grads_ref[pair, 0] for pair in range(PAIRS)], axis=1)
    unweave(section_ref, dot_rows(n1_ref[...], rows).astype(BF), keep_ref, away_ref)
    acc[...] += dot_columns(rows, weave(section_ref, mine_ref, other_ref))

    @pl.when(step == 0)
    def _():
        dvec_ref[2:3, :] = column_sums(rows.astype(F32))

    @pl.when(step == 2)
    def _():
        dvec_ref[3:4, :] = column_sums(rows.astype(F32))
        dn1 = acc[...]
        unit, scale = normalized(x_ref[...].astype(F32))
        dx_ref[...] = (dx1_ref[...] + norm_back(dn1, vec_ref[0:1, :], unit, scale)).astype(BF)
        dvec_ref[0:1, :] = column_sums(dn1 * unit)
        dvec_ref[1:2, :] = column_sums(dn1)


def whole(*shape):
    return pl.BlockSpec(shape, lambda *_: (0,) * len(shape))


def stepped(*shape):
    return pl.BlockSpec(shape, lambda step: (step,) + (0,) * (len(shape) - 1))


def out(shape, kind):
    return jax.ShapeDtypeStruct(shape, kind)


def params():
    return pltpu.CompilerParams(vmem_limit_bytes=VMEM_BYTES)


def cost(us):
    return pl.CostEstimate(
        flops=int(us * 4e8), bytes_accessed=int(us * 3e6), transcendentals=0
    )


def middle(rows):
    return rows // 32 * 16


def sum_pairs_kernel(*refs):
    zero_ref, one_ref, minus_ref, low_ref, high_ref, total = refs[-6:]
    pairs = refs[:-6]
    y = lax.rem(lax.axis_index("replica"), 4)
    rows, half = zero_ref.shape[1], low_ref.shape[1]
    row = 0
    for keep, got in zip(pairs[::2], pairs[1::2]):
        total[row : row + keep.shape[1], :] = add(keep[0], got[0]).astype(BF)
        row += keep.shape[1]
    if row < total.shape[0]:
        total[row:, :] = jnp.zeros((total.shape[0] - row, WIDTH), BF)

    def piece(k):
        return total[pl.ds(pl.multiple_of(lax.rem(y + k, 4) * rows, 16), rows), :]

    zero_ref[0] = piece(0)
    one_ref[0] = piece(1)
    minus_ref[0] = piece(3)
    two = piece(2)
    low_ref[0] = two[:half]
    high_ref[0] = two[half:]


def sum_pairs(pairs):
    rows = (sum(keep.shape[1] for keep, _ in pairs) + 63) // 64 * 16
    half = middle(rows)
    specs = [
        pl.BlockSpec((1, keep.shape[1], WIDTH), lambda step: (step, 0, 0))
        for keep, _ in pairs
        for _ in range(2)
    ]
    shapes = [(GROUPS, count, WIDTH) for count in (rows, rows, rows, half, rows - half)]
    return pl.pallas_call(
        sum_pairs_kernel,
        grid=(GROUPS,),
        in_specs=specs,
        out_specs=[stepped(1, *shape[1:]) for shape in shapes],
        out_shape=[out(shape, BF) for shape in shapes],
        scratch_shapes=[pltpu.VMEM((4 * rows, WIDTH), BF)],
        compiler_params=params(),
        cost_estimate=cost(5),
        name="sum_pairs",
    )(*(value for pair in pairs for value in pair))


def sum_pairs_z_kernel(*refs):
    own_ref, low_ref, high_ref = refs[-3:]
    pairs = refs[:-3]
    on_first = lax.axis_index("group") % 2 == 0
    cut = low_ref.shape[1]
    total = [add(keep[...], got[...]).astype(BF) for keep, got in zip(pairs[::2], pairs[1::2])]
    total = jnp.concatenate(total, axis=1) if len(total) > 1 else total[0]
    own_ref[0] = lax.select(on_first, total[0], total[1])
    away = lax.select(on_first, total[1], total[0])
    low_ref[0] = away[:cut]
    high_ref[0] = away[cut:]


def sum_pairs_z(pairs):
    rows = sum(keep.shape[1] for keep, _ in pairs)
    cut = middle(rows)
    specs = [
        pl.BlockSpec((2, keep.shape[1], WIDTH), lambda step: (step, 0, 0))
        for keep, _ in pairs
        for _ in range(2)
    ]
    return pl.pallas_call(
        sum_pairs_z_kernel,
        grid=(4,),
        in_specs=specs,
        out_specs=[stepped(1, rows, WIDTH), stepped(1, cut, WIDTH), stepped(1, rows - cut, WIDTH)],
        out_shape=[
            out((4, rows, WIDTH), BF),
            out((4, cut, WIDTH), BF),
            out((4, rows - cut, WIDTH), BF),
        ],
        compiler_params=params(),
        cost_estimate=cost(5),
        name="sum_pairs_z",
    )(*(value for pair in pairs for value in pair))


def sum_y_kernel(zero_ref, one_ref, minus_ref, own_ref, low_ref, high_ref):
    z = lax.axis_index("group") % 2
    cut = low_ref.shape[1]

    def total(at):
        return (add(zero_ref[at], one_ref[at]) + minus_ref[at].astype(F32)).astype(BF)

    for x in range(4):
        own_ref[x] = total(2 * x + z)
        away = total(2 * x + 1 - z)
        low_ref[x] = away[:cut]
        high_ref[x] = away[cut:]


def sum_y(zero, one, minus):
    rows = zero.shape[1]
    cut = middle(rows)
    vmem = pl.BlockSpec(memory_space=pltpu.VMEM)
    return pl.pallas_call(
        sum_y_kernel,
        in_specs=[vmem] * 3,
        out_specs=[vmem] * 3,
        out_shape=[
            out((4, rows, WIDTH), BF),
            out((4, cut, WIDTH), BF),
            out((4, rows - cut, WIDTH), BF),
        ],
        compiler_params=params(),
        cost_estimate=cost(4),
        name="sum_y",
    )(zero, one, minus)


def sum_z_kernel(own_ref, low_ref, high_ref, zero_ref, one_ref, minus_ref, two_low_ref, two_high_ref):
    x = lax.axis_index("group") // 2
    cut, half = low_ref.shape[1], two_low_ref.shape[0]

    def piece(k):
        at = lax.rem(x + k, 4)
        from_z = jnp.concatenate([low_ref[at], high_ref[at]], axis=0)
        return add(own_ref[at], from_z).astype(BF)

    zero_ref[...] = piece(0)
    one_ref[...] = piece(1)
    minus_ref[...] = piece(3)
    two = piece(2)
    two_low_ref[...] = two[:half]
    two_high_ref[...] = two[half:]


def sum_z(own, low, high):
    rows = own.shape[1]
    half = middle(rows)
    vmem = pl.BlockSpec(memory_space=pltpu.VMEM)
    return pl.pallas_call(
        sum_z_kernel,
        in_specs=[vmem] * 3,
        out_specs=[vmem] * 5,
        out_shape=[out((rows, WIDTH), BF)] * 3 + [out((half, WIDTH), BF), out((rows - half, WIDTH), BF)],
        compiler_params=params(),
        cost_estimate=cost(4),
        name="sum_z",
    )(own, low, high)


def sum_far_kernel(one_ref, minus_ref, left_ref, right_ref, one_out, minus_out):
    half = left_ref.shape[-2]
    one_out[..., :half, :] = add(one_ref[..., :half, :], left_ref[...]).astype(BF)
    one_out[..., half:, :] = one_ref[..., half:, :]
    minus_out[..., :half, :] = minus_ref[..., :half, :]
    minus_out[..., half:, :] = add(minus_ref[..., half:, :], right_ref[...]).astype(BF)


def sum_far(one, minus, from_left, from_right):
    vmem = pl.BlockSpec(memory_space=pltpu.VMEM)
    return pl.pallas_call(
        sum_far_kernel,
        in_specs=[vmem] * 4,
        out_specs=[vmem] * 2,
        out_shape=[out(one.shape, BF)] * 2,
        compiler_params=params(),
        cost_estimate=cost(2),
        name="sum_far",
    )(one, minus, from_left, from_right)


SMEM_SPEC = pl.BlockSpec(memory_space=pltpu.SMEM)
HEADS_SPEC = pl.BlockSpec((GROUPS, 1, ROWS, 128), lambda step: (0, step, 0, 0))
WIDE_SPEC = pl.BlockSpec((GROUPS, HALF, WIDTH), lambda step: (0, step, 0))
OUT_SPEC = pl.BlockSpec((GROUPS, HALF, WIDTH), lambda step: (0, 3, 0))
PROJ_SPEC = pl.BlockSpec((2, 4 * HALF, WIDTH), lambda step: (step, 1, 0))
DPROJ_SPEC = pl.BlockSpec((2, 4 * HALF, WIDTH), lambda step: (step, 0, 0))


def run_pre_forward(section, x, vec, slim):
    return pl.pallas_call(
        pre_forward,
        grid=(3,),
        in_specs=[SMEM_SPEC, whole(ROWS, WIDTH), whole(12, WIDTH), WIDE_SPEC, WIDE_SPEC],
        out_specs=[whole(ROWS, WIDTH), HEADS_SPEC],
        out_shape=[out((ROWS, WIDTH), BF), out((GROUPS, 3, ROWS, 128), BF)],
        compiler_params=params(),
        cost_estimate=cost(4),
        name="pre_forward",
    )(section, x, vec, *slim)


def run_attend_forward(length_row, qkv):
    return pl.pallas_call(
        attend_forward,
        grid=(1,),
        in_specs=[SMEM_SPEC, whole(GROUPS, 3, ROWS, 128)],
        out_specs=[whole(GROUPS, ROWS, 128), whole(SEQ, 128)],
        out_shape=[out((GROUPS, ROWS, 128), BF), out((SEQ, 128), F32)],
        compiler_params=params(),
        cost_estimate=cost(8),
        name="attend_forward",
    )(length_row, qkv)


def run_attend_backward(length_row, qkv, grad, logsum):
    return pl.pallas_call(
        attend_backward,
        grid=(1,),
        in_specs=[
            SMEM_SPEC,
            whole(GROUPS, 3, ROWS, 128),
            whole(GROUPS, ROWS, 128),
            whole(SEQ, 128),
        ],
        out_specs=whole(GROUPS, 3, ROWS, 128),
        out_shape=out((GROUPS, 3, ROWS, 128), BF),
        scratch_shapes=[pltpu.VMEM((SEQ, 128), F32), pltpu.VMEM((SEQ, 128), F32)],
        compiler_params=params(),
        cost_estimate=cost(16),
        name="attend_backward",
    )(length_row, qkv, grad, logsum)


def run_post_forward(section, mixed, x, vec, slim, wide):
    return pl.pallas_call(
        post_forward,
        grid=(4,),
        in_specs=[
            SMEM_SPEC,
            whole(GROUPS, ROWS, 128),
            whole(ROWS, WIDTH),
            whole(12, WIDTH),
            OUT_SPEC,
            OUT_SPEC,
            WIDE_SPEC,
            WIDE_SPEC,
            PROJ_SPEC,
            PROJ_SPEC,
        ],
        out_specs=[
            whole(ROWS, WIDTH),
            whole(ROWS, WIDTH),
            whole(ROWS, WIDTH),
            stepped(1, ROWS, WIDTH),
        ],
        out_shape=[
            out((ROWS, WIDTH), BF),
            out((ROWS, WIDTH), F32),
            out((ROWS, WIDTH), BF),
            out((4, ROWS, WIDTH), F32),
        ],
        scratch_shapes=[pltpu.VMEM((ROWS, WIDTH), F32)],
        compiler_params=params(),
        cost_estimate=cost(8),
        name="post_forward",
    )(section, mixed, x, vec, *slim, *wide, *wide)


def run_post_backward(section, dy, u, n2, x1, mixed, vec, slim, wide):
    return pl.pallas_call(
        post_backward,
        grid=(4,),
        in_specs=[
            SMEM_SPEC,
            whole(ROWS, WIDTH),
            stepped(1, ROWS, WIDTH),
            whole(ROWS, WIDTH),
            whole(ROWS, WIDTH),
            whole(GROUPS, ROWS, 128),
            whole(12, WIDTH),
            OUT_SPEC,
            OUT_SPEC,
            WIDE_SPEC,
            WIDE_SPEC,
            PROJ_SPEC,
            PROJ_SPEC,
        ],
        out_specs=[
            whole(ROWS, WIDTH),
            whole(GROUPS, ROWS, 128),
            whole(12, WIDTH),
            whole(GROUPS, HALF, WIDTH),
            whole(GROUPS, HALF, WIDTH),
            WIDE_SPEC,
            WIDE_SPEC,
            DPROJ_SPEC,
            DPROJ_SPEC,
        ],
        out_shape=[
            out((ROWS, WIDTH), F32),
            out((GROUPS, ROWS, 128), BF),
            out((12, WIDTH), F32),
            out((GROUPS, HALF, WIDTH), BF),
            out((GROUPS, HALF, WIDTH), BF),
            out((GROUPS, 4 * HALF, WIDTH), BF),
            out((GROUPS, 4 * HALF, WIDTH), BF),
            out((GROUPS, 4 * HALF, WIDTH), BF),
            out((GROUPS, 4 * HALF, WIDTH), BF),
        ],
        scratch_shapes=[pltpu.VMEM((ROWS, WIDTH), F32)],
        compiler_params=params(),
        cost_estimate=cost(14),
        name="post_backward",
    )(section, dy, u, n2, x1, mixed, vec, *slim, *wide, *wide)


def run_pre_backward(section, grads, n1, x, dx1, vec, slim):
    return pl.pallas_call(
        pre_backward,
        grid=(3,),
        in_specs=[
            SMEM_SPEC,
            HEADS_SPEC,
            whole(ROWS, WIDTH),
            whole(ROWS, WIDTH),
            whole(ROWS, WIDTH),
            whole(12, WIDTH),
            WIDE_SPEC,
            WIDE_SPEC,
        ],
        out_specs=[whole(ROWS, WIDTH), whole(12, WIDTH), WIDE_SPEC, WIDE_SPEC],
        out_shape=[
            out((ROWS, WIDTH), BF),
            out((12, WIDTH), F32),
            out((GROUPS, 3 * HALF, WIDTH), BF),
            out((GROUPS, 3 * HALF, WIDTH), BF),
        ],
        scratch_shapes=[pltpu.VMEM((ROWS, WIDTH), F32)],
        compiler_params=params(),
        cost_estimate=cost(8),
        name="pre_backward",
    )(section, grads, n1, x, dx1, vec, *slim)


def exchange(value):
    return lax.all_to_all(value, "group", 0, 0, tiled=True)


def body(
    tokens,
    cotangent,
    lengths,
    ln1_gain,
    ln1_bias,
    w_qkv,
    b_query,
    b_value,
    w_out,
    b_out,
    ln2_gain,
    ln2_bias,
    w_fc,
    b_fc,
    w_proj,
    b_proj,
):
    section = lax.axis_index("section")
    which = section.astype(jnp.int32).reshape(1)
    length_row = lax.dynamic_index_in_dim(lengths, section, 0, keepdims=False)
    tokens_row = lax.dynamic_index_in_dim(tokens, section, 0, keepdims=False)

    vectors = (ln1_gain, ln1_bias, b_query, b_value, b_out, ln2_gain, ln2_bias, b_proj)
    keep, away = run_pack_shard(which, w_qkv, w_out, w_fc, w_proj, b_fc, *vectors)
    got = swap(away)
    shard_zero, shard_one = pick(keep, got), pick(got, keep)
    front = SLIM + VEC_ROWS
    slim_zero = Gather(jnp.concatenate([shard_zero[:front], shard_one[SLIM:front]], axis=0))
    wide_zero = Gather(shard_zero[front:])
    slim_one = Gather(shard_one[:SLIM])
    wide_one = Gather(shard_one[front:])

    slim_zero.near()
    wide_zero.shard = slim_zero.after(wide_zero.shard)
    slim_zero.far()
    wide_zero.shard = slim_zero.after(wide_zero.shard)
    slim_zero.last()
    wide_zero.near()
    mine = slim_zero.whole()
    slim = mine, swap(mine)
    vecs = run_unpack_vectors(mine)

    n1, send = run_pre_forward(which, tokens_row, vecs[0], slim)
    send = wide_zero.after(send)
    slim_one.shard, send = tie(slim_one.shard, send)
    wide_zero.far()
    slim_one.near()
    heads = exchange(send)
    heads = wide_zero.after(heads)
    heads = slim_one.after(heads)
    wide_zero.last()
    slim_one.far()
    mixed, logsum = run_attend_forward(length_row, heads)
    mixed = wide_zero.after(mixed)
    mixed = slim_one.after(mixed)
    slim_one.last()
    mine = wide_zero.whole()
    wide = mine, swap(mine)
    mixed = exchange(mixed)
    mixed = slim_one.after(mixed)
    wide_one.shard, mixed = tie(wide_one.shard, mixed)
    wide_one.near()
    mine = slim_one.whole()
    slim_next = mine, swap(mine)
    result, x1, n2, u = run_post_forward(which, mixed, tokens_row, vecs[0], slim, wide)
    kept_zero = (tokens_row, n1, heads, logsum, mixed, x1, n2, u, slim, wide)

    output_zero = result
    slim = slim_next
    n1, send = run_pre_forward(which, result, vecs[1], slim)
    send = wide_one.after(send)
    wide_one.far()
    heads = exchange(send)
    heads = wide_one.after(heads)
    wide_one.last()
    mine = wide_one.whole()
    wide = mine, swap(mine)
    mixed, logsum = run_attend_forward(length_row, heads)
    mixed = exchange(mixed)
    output_one, x1, n2, u = run_post_forward(which, mixed, result, vecs[1], slim, wide)
    kept_one = (result, n1, heads, logsum, mixed, x1, n2, u, slim, wide)

    def first_part(layer, grad, kept):
        _, _, _, _, mixed, x1, n2, u, slim, wide = kept
        dx1, send, dvec, *halves = run_post_backward(
            which, grad, u, n2, x1, mixed, vecs[layer], slim, wide
        )
        pairs = [(keep, swap(away)) for keep, away in zip(halves[::2], halves[1::2])]
        return dx1, send, dvec, pairs

    def second_part(layer, dheads, dx1, kept):
        rows, n1, _, _, _, _, _, _, slim, _ = kept
        grad, dvec, keep, away = run_pre_backward(which, dheads, n1, rows, dx1, vecs[layer], slim)
        return grad, dvec, (keep, swap(away))

    far = ("from_left", "from_right")
    near = ("zero", "one", "minus")
    grad = lax.dynamic_index_in_dim(cotangent, section, 0, keepdims=False)
    dx1, send, dvec_two, pairs = first_part(1, grad, kept_one)
    bulk_one = BulkSum(pairs)
    bulk_one.y_far()
    dheads = run_attend_backward(length_row, kept_one[2], exchange(send), kept_one[3])
    dheads = exchange(dheads)
    dheads = after(bulk_one, far, dheads)
    bulk_one.y_near()
    grad_one, dvec_one, slim_pair = second_part(1, dheads, dx1, kept_one)
    dvec_last = dvec_one + dvec_two

    dx1, send, dvec_two, pairs = first_part(0, grad_one, kept_zero)
    pairs = [*pairs, slim_pair]
    grad_heads = exchange(send)
    *keeps, grad_heads = tie(*(keep for keep, _ in pairs), grad_heads)
    bulk = GroupSum([(keep, got) for keep, (_, got) in zip(keeps, pairs)])
    dheads = run_attend_backward(length_row, kept_zero[2], grad_heads, kept_zero[3])
    dheads = after(bulk_one, near, dheads)
    bulk_one.over_z()
    dheads = exchange(dheads)
    dheads = after(bulk, ("own", "low", "high"), dheads)
    dheads = after(bulk_one, ("own", "low", "high"), dheads)
    bulk.far()
    bulk_one.x_far()
    grad_zero, dvec_one, (keep, got) = second_part(0, dheads, dx1, kept_zero)
    dvecs = jnp.stack([dvec_one + dvec_two, dvec_last])
    last = run_pack_last(keep, got, dvecs, swap(dvecs))
    last = after(bulk, far, last)
    last = after(bulk_one, far, last)
    bulk.near()
    piece = last.shape[1] // 8
    arrived = lax.all_to_all(
        last.reshape(64, piece, WIDTH), ("group", "replica"), 0, 0, tiled=True
    )
    y = lax.rem(lax.axis_index("replica"), 4)
    quarter = bulk.zero.shape[0] // 4
    ring = RingSum(bulk.total().astype(BF).reshape(4, quarter, WIDTH), y, along_y)
    ring.far()
    bulk_one.x_near()
    ring.near()
    after(bulk_one, near, arrived)
    arrived = after(ring, ("one", "minus"), arrived)
    both, last = every_part(
        jnp.concatenate([ring.total(), bulk_one.total()], axis=0),
        jnp.sum(arrived.astype(F32), axis=0).astype(BF),
    )
    bulk, sum_one = both[:, :quarter].reshape(-1, WIDTH), both[:, quarter:].reshape(-1, WIDTH)
    split = HALF + WIDE
    sum_one = sum_one[:split]

    def own_layer(zero, one):
        mine, other = pick(zero, one), swap(pick(one, zero))
        return pick(mine, other).astype(F32), pick(other, mine).astype(F32)

    first, second = own_layer(bulk[:split], sum_one)
    first_slim, second_slim = own_layer(last[: 3 * HALF], bulk[split:])

    def block(low, high, j):
        at = slice(HALF * j, HALF * j + HALF)
        return jnp.concatenate([low[at], high[at]], axis=0)

    grad_qkv = jnp.concatenate([block(first_slim, second_slim, j) for j in range(3)], axis=1)
    grad_out = block(first, second, 0)
    grad_fc = jnp.concatenate([block(first, second, 1 + j) for j in range(4)], axis=1)
    grad_proj = jnp.concatenate([first[5 * HALF :], second[5 * HALF :]], axis=0)
    v = last[3 * HALF :].astype(F32)
    v = pick(v[:VEC_ROWS], v[VEC_ROWS:])

    def both_micro(zero, one):
        mine, other = pick(zero, one), swap(pick(one, zero))
        return jnp.stack([pick(mine, other), pick(other, mine)])[None]

    acts = both_micro(output_zero, output_one)
    in_grads = both_micro(grad_zero, grad_one)
    return (
        acts,
        in_grads,
        v[0:1, :SHARD],
        v[1:2, :SHARD],
        grad_qkv[None],
        v[2:3, :SHARD],
        v[3:4, :SHARD],
        grad_out[None],
        v[4:5, :SHARD],
        v[5:6, :SHARD],
        v[6:7, :SHARD],
        grad_fc[None],
        v[8:9, : 4 * SHARD],
        grad_proj[None],
        v[7:8, :SHARD],
    )


def solution(mesh):
    placed = (
        P("replica", "group", None),
        P("replica", "group", None),
        P("replica", None),
        P("section", "group"),
        P("section", "group"),
        P("section", "group", None),
        P("section", "group"),
        P("section", "group"),
        P("section", "group", None),
        P("section", "group"),
        P("section", "group"),
        P("section", "group"),
        P("section", "group", None),
        P("section", "group"),
        P("section", "group", None),
        P("section", "group"),
    )
    return jax.shard_map(
        body,
        mesh=mesh,
        in_specs=placed,
        out_specs=(
            P("section", "replica", "group", None),
            P("section", "replica", "group", None),
            P("section", "group"),
            P("section", "group"),
            P("section", "group", None),
            P("section", "group"),
            P("section", "group"),
            P("section", "group", None),
            P("section", "group"),
            P("section", "group"),
            P("section", "group"),
            P("section", "group", None),
            P("section", "group"),
            P("section", "group", None),
            P("section", "group"),
        ),
        check_vma=False,
    )
```

```python
import functools

import jax
import jax.numpy as jnp
from jax import lax
from jax.experimental import pallas as pl
from jax.experimental.pallas import tpu as pltpu
from jax.sharding import PartitionSpec as P

WIDTH = 768
GROUPS = 8
PAIRS = 6
SEQ = 1024
ROWS = 128
BLOCK = 256
SHARD = 96
HALF = 48
SLIM = 192
WIDE = 384
VEC_ROWS = 16
EPSILON = 1e-05
VMEM_BYTES = 40 * 1024 * 1024
GELU_C = 0.7978845608028654
BF = jnp.bfloat16
F32 = jnp.float32


def torus_pairs(move):
    pairs = []
    for source in range(64):
        group, replica = divmod(source, 8)
        x, z_lo = divmod(group, 2)
        z_hi, y = divmod(replica, 4)
        x, y, z = move(x, y, z_hi * 2 + z_lo)
        pairs.append((source, ((x % 4) * 2 + z % 2) * 8 + (z % 4) // 2 * 4 + y % 4))
    return pairs


def along_x(value, by):
    return lax.ppermute(value, ("group", "replica"), torus_pairs(lambda x, y, z: (x + by, y, z)))


def along_y(value, by):
    return lax.ppermute(value, ("group", "replica"), torus_pairs(lambda x, y, z: (x, y + by, z)))


def along_z(value, by):
    return lax.ppermute(value, ("group", "replica"), torus_pairs(lambda x, y, z: (x, y, z + by)))


def swap(value):
    return lax.ppermute(value, "section", [(0, 1), (1, 0)])


def tie(*values):
    return lax.optimization_barrier(values)


def pick(on_first, on_second):
    return jnp.where(lax.axis_index("section") == 0, on_first, on_second)


def after(holder, names, value):
    tied = tie(*(getattr(holder, name) for name in names), value)
    for name, part in zip(names, tied):
        setattr(holder, name, part)
    return tied[-1]


class Gather:
    def __init__(self, shard):
        self.shard = shard
        self.cut = shard.shape[0] // 2

    def near(self):
        shard, cut = self.shard, self.cut
        self.left = along_x(shard, 1)
        self.right = along_x(shard, -1)
        self.z_low = along_z(shard[:cut], 1)
        self.z_high = along_z(shard[cut:], -1)

    def far(self):
        cut = self.cut
        self.far_low = along_x(self.left[:cut], 1)
        self.far_high = along_x(self.right[cut:], -1)
        self.z_left = along_z(self.left, 1)
        self.z_right = along_z(self.right, -1)

    def last(self):
        self.z_far_low = along_z(self.far_low, 1)
        self.z_far_high = along_z(self.far_high, -1)

    def after(self, *values):
        names = [name for name in vars(self) if name not in ("cut",)]
        count = len(names)
        tied = tie(*(getattr(self, name) for name in names), *values)
        for name, value in zip(names, tied):
            setattr(self, name, value)
        return tied[count:] if len(values) != 1 else tied[count]

    def whole(self):
        pieces = (
            self.shard,
            self.left,
            self.right,
            self.far_low,
            self.far_high,
            self.z_low,
            self.z_high,
            self.z_left,
            self.z_right,
            self.z_far_low,
            self.z_far_high,
        )
        return assemble(self.cut, *pieces)


def add(left, right):
    return left.astype(F32) + right.astype(F32)


class GroupSum:
    def __init__(self, pairs):
        self.own, away_low, away_high = sum_pairs_z(pairs)
        self.low = along_z(away_low, 1)
        self.high = along_z(away_high, -1)

    def far(self):
        self.zero, self.one, self.minus, two_low, two_high = sum_z(self.own, self.low, self.high)
        self.from_left = along_x(two_low, 1)
        self.from_right = along_x(two_high, -1)

    def near(self):
        one, minus = sum_far(self.one, self.minus, self.from_left, self.from_right)
        self.one = along_x(one, 1)
        self.minus = along_x(minus, -1)

    def total(self):
        return self.zero.astype(F32) + self.one.astype(F32) + self.minus.astype(F32)


class DirectSum:
    def __init__(self, parts, place, along):
        def piece(k):
            return lax.dynamic_index_in_dim(parts, lax.rem(place + k, 4), 0, keepdims=False)

        self.zero = piece(0)
        self.one = along(piece(1), 1)
        self.minus = along(piece(3), -1)
        self.two = along(piece(2), 2)

    def total(self):
        return add(self.zero, self.two) + add(self.one, self.minus)


class BulkSum:
    def __init__(self, pairs):
        self.zero, self.one, self.minus, self.two_low, self.two_high = sum_pairs(pairs)

    def y_far(self):
        self.from_left = along_y(self.two_low, 1)
        self.from_right = along_y(self.two_high, -1)

    def y_near(self):
        one, minus = sum_far(self.one, self.minus, self.from_left, self.from_right)
        self.one = along_y(one, 1)
        self.minus = along_y(minus, -1)

    def over_z(self):
        self.own, low, high = sum_y(self.zero, self.one, self.minus)
        self.low = along_z(low, 1)
        self.high = along_z(high, -1)

    def x_far(self):
        self.zero, self.one, self.minus, two_low, two_high = sum_z(self.own, self.low, self.high)
        self.from_left = along_x(two_low, 1)
        self.from_right = along_x(two_high, -1)

    def x_near(self):
        one, minus = sum_far(self.one, self.minus, self.from_left, self.from_right)
        self.one = along_x(one, 1)
        self.minus = along_x(minus, -1)

    def total(self):
        return self.zero.astype(F32) + self.one.astype(F32) + self.minus.astype(F32)

def every_part(total, whole):
    z_hi, y = jnp.divmod(lax.axis_index("replica"), 4)
    rows, piece = total.shape[0], whole.shape[0]
    mine = jnp.concatenate([total.astype(BF), whole], axis=0)
    other = along_z(mine, 2)
    both = add(mine[:rows], other[:rows]).astype(BF)
    first, second = mine[rows:], other[rows:]
    first, second = jnp.where(z_hi == 0, first, second), jnp.where(z_hi == 0, second, first)
    mine = jnp.concatenate([both, first, second], axis=0)
    half = mine.shape[0] // 2
    left = along_y(mine, 1)
    right = along_y(mine, -1)
    far = jnp.concatenate([along_y(left[:half], 1), along_y(right[half:], -1)], axis=0)
    full = jnp.zeros((4,) + mine.shape, BF)
    for part, k in ((mine, 0), (left, 3), (right, 1), (far, 2)):
        full = lax.dynamic_update_slice(full, part[None], (lax.rem(y + k, 4), 0, 0))
    last = full[:, rows:].reshape(4, 2, piece, WIDTH).transpose(1, 0, 2, 3)
    return full[:, :rows], last.reshape(-1, WIDTH)


def dot(left, right):
    return jnp.dot(left, right, preferred_element_type=F32)


def dot_rows(left, right):
    return lax.dot_general(left, right, (((0,), (0,)), ((), ())), preferred_element_type=F32)


def dot_columns(left, right):
    return lax.dot_general(left, right, (((1,), (1,)), ((), ())), preferred_element_type=F32)


def normalized(rows):
    center = rows - jnp.mean(rows, axis=-1, keepdims=True)
    scale = lax.rsqrt(jnp.mean(center * center, axis=-1, keepdims=True) + EPSILON)
    return center * scale, scale


def norm_back(grad, gain, unit, scale):
    inner = grad * gain
    return scale * (
        inner
        - jnp.mean(inner, axis=-1, keepdims=True)
        - unit * jnp.mean(inner * unit, axis=-1, keepdims=True)
    )


def column_sums(rows):
    return jnp.sum(rows, axis=0, keepdims=True)


PLACES = (
    (0, False, False),
    (3, False, False),
    (1, False, False),
    (2, False, False),
    (2, False, True),
    (0, True, False),
    (0, True, True),
    (3, True, False),
    (1, True, False),
    (2, True, False),
    (2, True, True),
)


def assemble_rows(cut, *refs):
    pieces, full = refs[: len(PLACES)], refs[len(PLACES)]
    group = lax.axis_index("group")
    x, z = group // 2, group % 2
    for piece, (dx, flip, high) in zip(pieces, PLACES):
        at = lax.rem(x + dx, 4) * 2 + (1 - z if flip else z)
        row = cut if high else 0
        full[pl.ds(at, 1), row : row + piece.shape[0]] = piece[...][None]


def assemble(cut, *pieces):
    rows = pieces[0].shape[0]
    return pl.pallas_call(
        functools.partial(assemble_rows, cut),
        in_specs=[pl.BlockSpec(memory_space=pltpu.VMEM)] * len(PLACES),
        out_specs=pl.BlockSpec(memory_space=pltpu.VMEM),
        out_shape=jax.ShapeDtypeStruct((GROUPS, rows, WIDTH), BF),
        compiler_params=pltpu.CompilerParams(vmem_limit_bytes=VMEM_BYTES),
        cost_estimate=cost(4),
        name="assemble",
    )(*pieces)


def pack_shard(section_ref, qkv_ref, out_ref, fc_ref, proj_ref, bias_ref, *refs):
    vectors, (keep_ref, away_ref) = refs[:8], refs[8:]
    on_first = section_ref[0] == 0

    def put(row, low, high):
        at = slice(row, row + low.shape[0])
        keep_ref[at, :] = lax.select(on_first, low, high)
        away_ref[at, :] = lax.select(on_first, high, low)

    for j in range(3):
        at = slice(WIDTH * j, WIDTH * (j + 1))
        put(HALF * j, qkv_ref[0, :HALF, at], qkv_ref[0, HALF:, at])
    put(3 * HALF, out_ref[0, :HALF], out_ref[0, HALF:])
    for j in range(4):
        at = slice(WIDTH * j, WIDTH * (j + 1))
        put(SLIM + VEC_ROWS + HALF * j, fc_ref[0, :HALF, at], fc_ref[0, HALF:, at])
    put(SLIM + VEC_ROWS + 4 * HALF, proj_ref[0, : 4 * HALF], proj_ref[0, 4 * HALF :])
    rows = jnp.concatenate([ref[...].astype(F32) for ref in vectors], axis=0)
    rows = jnp.concatenate([rows, jnp.zeros((8, WIDTH - SHARD), F32)], axis=1)
    bias = jnp.concatenate([bias_ref[...].astype(F32), jnp.zeros((1, WIDTH // 2), F32)], axis=1)
    rows = jnp.concatenate([rows, bias, jnp.zeros((7, WIDTH), F32)], axis=0).astype(BF)
    put(SLIM, rows, rows)


def run_pack_shard(section, qkv, out_w, fc, proj, bias, *vectors):
    shape = jax.ShapeDtypeStruct((SLIM + VEC_ROWS + WIDE, WIDTH), BF)
    return pl.pallas_call(
        pack_shard,
        grid=(1,),
        in_specs=[pl.BlockSpec(memory_space=pltpu.SMEM)]
        + [whole(*value.shape) for value in (qkv, out_w, fc, proj, bias, *vectors)],
        out_specs=[whole(*shape.shape)] * 2,
        out_shape=[shape, shape],
        compiler_params=pltpu.CompilerParams(vmem_limit_bytes=VMEM_BYTES),
        cost_estimate=cost(3),
        name="pack_shard",
    )(section, qkv, out_w, fc, proj, bias, *vectors)


def one_hot(group):
    row = lax.broadcasted_iota(jnp.int32, (128, WIDTH), 0)
    lane = lax.broadcasted_iota(jnp.int32, (128, WIDTH), 1)
    return jnp.where((lane == row + SHARD * group) & (row < SHARD), 1.0, 0.0).astype(BF)


def unpack_vectors(mine_ref, vecs_ref):
    total = jnp.zeros((2 * VEC_ROWS, WIDTH), F32)
    for group in range(GROUPS):
        total = total + dot(mine_ref[group, :, :128], one_hot(group))
    for layer in range(2):
        vecs_ref[layer, 0:8, :] = total[VEC_ROWS * layer : VEC_ROWS * layer + 8]
        for j in range(4):
            for side in range(2):
                piece = mine_ref[2 * j + side, VEC_ROWS * layer : VEC_ROWS * (layer + 1), : WIDTH // 2]
                at = slice(side * (WIDTH // 2), (side + 1) * (WIDTH // 2))
                vecs_ref[layer, 8 + j : 9 + j, at] = piece.astype(F32)[8:9]


def run_unpack_vectors(mine):
    return pl.pallas_call(
        unpack_vectors,
        grid=(1,),
        in_specs=[pl.BlockSpec((GROUPS, 2 * VEC_ROWS, WIDTH), lambda step: (0, SLIM // (2 * VEC_ROWS), 0))],
        out_specs=whole(2, 12, WIDTH),
        out_shape=jax.ShapeDtypeStruct((2, 12, WIDTH), F32),
        cost_estimate=cost(2),
        name="unpack_vectors",
    )(mine)


def pack_last(keep_ref, got_ref, vecs_ref, other_vecs_ref, out_ref):
    rows = keep_ref.shape[1]
    for group in range(GROUPS):
        out_ref[group, :rows] = add(keep_ref[group], got_ref[group]).astype(BF)
        for layer in range(2):
            plain = vecs_ref[layer, 0:8, :] + other_vecs_ref[layer, 0:8, :]
            plain = lax.dot_general(
                plain.astype(BF), one_hot(group), (((1,), (1,)), ((), ())), preferred_element_type=F32
            )
            plain = jnp.concatenate([plain, jnp.zeros((8, WIDTH - 128), F32)], axis=1)
            side = group % 2
            at = slice(side * (WIDTH // 2), (side + 1) * (WIDTH // 2))
            row = slice(8 + group // 2, 9 + group // 2)
            bias = vecs_ref[layer, row, at] + other_vecs_ref[layer, row, at]
            bias = jnp.concatenate([bias, jnp.zeros((1, WIDTH // 2), F32)], axis=1)
            plain = jnp.concatenate([plain, bias, jnp.zeros((7, WIDTH), F32)], axis=0)
            low = rows + VEC_ROWS * layer
            out_ref[group, low : low + VEC_ROWS] = plain.astype(BF)


def run_pack_last(keep, got, vecs, other_vecs):
    vmem = pl.BlockSpec(memory_space=pltpu.VMEM)
    rows = keep.shape[1] + 2 * VEC_ROWS
    return pl.pallas_call(
        pack_last,
        in_specs=[vmem] * 4,
        out_specs=vmem,
        out_shape=jax.ShapeDtypeStruct((GROUPS, rows, WIDTH), BF),
        compiler_params=pltpu.CompilerParams(vmem_limit_bytes=VMEM_BYTES),
        cost_estimate=cost(3),
        name="pack_last",
    )(keep, got, vecs, other_vecs)


def put_pairs(ref, rows, *index):
    for pair in range(PAIRS):
        ref[(pair, *index)] = rows[:, pair * 128 : (pair + 1) * 128]
    for pair in range(PAIRS, GROUPS):
        ref[(pair, *index)] = jnp.zeros((ROWS, 128), BF)


def weave(section_ref, mine_ref, other_ref):
    on_first = section_ref[0] == 0
    mine, other = mine_ref[...], other_ref[...]
    both = [lax.select(on_first, mine, other), lax.select(on_first, other, mine)]
    return jnp.concatenate(both, axis=1).reshape(WIDTH, WIDTH)


def unweave(section_ref, rows, keep_ref, away_ref):
    on_first = section_ref[0] == 0
    groups, half, _ = keep_ref.shape
    rows = rows.reshape(groups, 2 * half, WIDTH)
    low, high = rows[:, :half], rows[:, half:]
    keep_ref[...] = lax.select(on_first, low, high)
    away_ref[...] = lax.select(on_first, high, low)


def pre_forward(section_ref, x_ref, vec_ref, mine_ref, other_ref, n1_ref, send_ref):
    step = pl.program_id(0)

    @pl.when(step == 0)
    def _():
        unit, _ = normalized(x_ref[...].astype(F32))
        n1_ref[...] = (unit * vec_ref[0:1, :] + vec_ref[1:2, :]).astype(BF)

    bias = jnp.where(step == 0, vec_ref[2:3, :], jnp.where(step == 2, vec_ref[3:4, :], 0.0))
    product = dot(n1_ref[...], weave(section_ref, mine_ref, other_ref))
    put_pairs(send_ref, (product + bias).astype(BF), 0)


def visible(length_ref, at, columns):
    first_end = length_ref[0]
    second_end = first_end + length_ref[1]
    row = lax.broadcasted_iota(jnp.int32, (BLOCK, 1), 0) + at
    start = jnp.where(row >= second_end, second_end, jnp.where(row >= first_end, first_end, 0))
    column = lax.broadcasted_iota(jnp.int32, (BLOCK, columns), 1)
    return (column >= start) & (column <= row)


def of_head(rows, head):
    lane = lax.broadcasted_iota(jnp.int32, rows.shape, 1)
    keep = lane < 64 if head == 0 else lane >= 64
    return jnp.where(keep, rows, jnp.zeros_like(rows))


def both_heads(first, second):
    lane = lax.broadcasted_iota(jnp.int32, first.shape, 1)
    return jnp.where(lane < 64, first, second)


def attend_forward(length_ref, qkv_ref, out_ref, logsum_ref):
    for block in range(SEQ // BLOCK):
        keys = (block + 1) * BLOCK
        query = qkv_ref[2 * block : 2 * block + 2, 0].reshape(BLOCK, 128)
        query = (query.astype(F32) * 0.125).astype(BF)
        key = qkv_ref[: 2 * block + 2, 1].reshape(keys, 128)
        value = qkv_ref[: 2 * block + 2, 2].reshape(keys, 128)
        allowed = visible(length_ref, block * BLOCK, keys)
        mixed, sums = [], []
        for head in range(2):
            scores = dot_columns(of_head(query, head), key)
            scores = jnp.where(allowed, scores, -1e30)
            maximum = jnp.max(scores, axis=-1, keepdims=True)
            expo = jnp.exp(scores - maximum)
            total = jnp.sum(expo, axis=-1, keepdims=True)
            mixed.append(dot((expo * (1.0 / total)).astype(BF), value))
            sums.append(jnp.broadcast_to(maximum + jnp.log(total), (BLOCK, 128)))
        out_ref[2 * block : 2 * block + 2] = both_heads(*mixed).astype(BF).reshape(2, 128, 128)
        logsum_ref[block * BLOCK : (block + 1) * BLOCK, :] = both_heads(*sums)


def attend_backward(length_ref, qkv_ref, grad_ref, logsum_ref, out_ref, key_acc, value_acc):
    key_acc[...] = jnp.zeros_like(key_acc)
    value_acc[...] = jnp.zeros_like(value_acc)
    for block in range(SEQ // BLOCK):
        keys = (block + 1) * BLOCK
        query = qkv_ref[2 * block : 2 * block + 2, 0].reshape(BLOCK, 128)
        query = (query.astype(F32) * 0.125).astype(BF)
        grad = grad_ref[2 * block : 2 * block + 2].reshape(BLOCK, 128)
        key = qkv_ref[: 2 * block + 2, 1].reshape(keys, 128)
        value = qkv_ref[: 2 * block + 2, 2].reshape(keys, 128)
        allowed = visible(length_ref, block * BLOCK, keys)
        grad_query = []
        for head in range(2):
            query_one, grad_one = of_head(query, head), of_head(grad, head)
            logsum = logsum_ref[block * BLOCK : (block + 1) * BLOCK, 64 * head : 64 * head + 1]
            scores = jnp.where(allowed, dot_columns(query_one, key), -1e30)
            probs = jnp.exp(scores - logsum)
            grad_probs = dot_columns(grad_one, value)
            delta = jnp.sum(probs * grad_probs, axis=-1, keepdims=True)
            grad_scores = (probs * (grad_probs - delta)).astype(BF)
            grad_query.append(dot(grad_scores, key))
            key_acc[:keys, :] += dot_rows(grad_scores, query_one)
            value_acc[:keys, :] += dot_rows(probs.astype(BF), grad_one)
        out = (both_heads(*grad_query) * 0.125).astype(BF)
        out_ref[2 * block : 2 * block + 2, 0] = out.reshape(2, 128, 128)
    out_ref[:, 1] = key_acc[...].astype(BF).reshape(GROUPS, 128, 128)
    out_ref[:, 2] = value_acc[...].astype(BF).reshape(GROUPS, 128, 128)


def post_forward(
    section_ref,
    mixed_ref,
    x_ref,
    vec_ref,
    out_mine,
    out_other,
    fc_mine,
    fc_other,
    proj_mine,
    proj_other,
    y_ref,
    x1_ref,
    n2_ref,
    u_ref,
    acc,
):
    step = pl.program_id(0)

    @pl.when(step == 0)
    def _():
        mixed = jnp.concatenate([mixed_ref[pair] for pair in range(PAIRS)], axis=1)
        x1 = x_ref[...].astype(F32) + dot(mixed, weave(section_ref, out_mine, out_other))
        x1 = x1 + vec_ref[4:5, :]
        x1_ref[...] = x1
        unit, _ = normalized(x1)
        n2_ref[...] = (unit * vec_ref[5:6, :] + vec_ref[6:7, :]).astype(BF)
        acc[...] = x1 + vec_ref[7:8, :]

    u = dot(n2_ref[...], weave(section_ref, fc_mine, fc_other)) + vec_ref[pl.ds(8 + step, 1), :]
    u_ref[0] = u
    active = 0.5 * u * (1.0 + jnp.tanh(GELU_C * (u + 0.044715 * (u * u * u))))
    acc[...] += dot(active.astype(BF), weave(section_ref, proj_mine, proj_other))

    @pl.when(step == 3)
    def _():
        y_ref[...] = acc[...].astype(BF)


def post_backward(
    section_ref,
    dy_ref,
    u_ref,
    n2_ref,
    x1_ref,
    mixed_ref,
    vec_ref,
    out_mine,
    out_other,
    fc_mine,
    fc_other,
    proj_mine,
    proj_other,
    dx1_ref,
    send_ref,
    dvec_ref,
    dout_keep,
    dout_away,
    dfc_keep,
    dfc_away,
    dproj_keep,
    dproj_away,
    acc,
):
    step = pl.program_id(0)
    dy = dy_ref[...].astype(F32)
    low = dy.astype(BF)

    @pl.when(step == 0)
    def _():
        acc[...] = jnp.zeros_like(acc)

    u = u_ref[0]
    square = u * u
    tanh = jnp.tanh(GELU_C * (u + 0.044715 * (square * u)))
    active = (0.5 * u * (1.0 + tanh)).astype(BF)
    slope = 0.5 * (1.0 + tanh) + 0.5 * u * (1.0 - tanh * tanh) * (
        GELU_C * (1.0 + 3.0 * 0.044715 * square)
    )
    du = (dot_columns(low, weave(section_ref, proj_mine, proj_other)) * slope).astype(BF)
    unweave(section_ref, dot_rows(active, low).astype(BF), dproj_keep, dproj_away)
    unweave(section_ref, dot_rows(n2_ref[...], du).astype(BF), dfc_keep, dfc_away)
    dvec_ref[pl.ds(8 + step, 1), :] = column_sums(du.astype(F32))
    acc[...] += dot_columns(du, weave(section_ref, fc_mine, fc_other))

    @pl.when(step == 3)
    def _():
        dn2 = acc[...]
        unit, scale = normalized(x1_ref[...])
        dx1 = dy + norm_back(dn2, vec_ref[5:6, :], unit, scale)
        dx1_ref[...] = dx1
        back = dx1.astype(BF)
        mixed = jnp.concatenate([mixed_ref[pair] for pair in range(PAIRS)], axis=1)
        unweave(section_ref, dot_rows(mixed, back).astype(BF), dout_keep, dout_away)
        put_pairs(send_ref, dot_columns(back, weave(section_ref, out_mine, out_other)).astype(BF))
        dvec_ref[0:4, :] = jnp.zeros((4, WIDTH), F32)
        dvec_ref[4:5, :] = column_sums(back.astype(F32))
        dvec_ref[5:6, :] = column_sums(dn2 * unit)
        dvec_ref[6:7, :] = column_sums(dn2)
        dvec_ref[7:8, :] = column_sums(low.astype(F32))


def pre_backward(
    section_ref,
    grads_ref,
    n1_ref,
    x_ref,
    dx1_ref,
    vec_ref,
    mine_ref,
    other_ref,
    dx_ref,
    dvec_ref,
    keep_ref,
    away_ref,
    acc,
):
    step = pl.program_id(0)

    @pl.when(step == 0)
    def _():
        acc[...] = jnp.zeros_like(acc)
        dvec_ref[...] = jnp.zeros_like(dvec_ref)

    rows = jnp.concatenate([grads_ref[pair, 0] for pair in range(PAIRS)], axis=1)
    unweave(section_ref, dot_rows(n1_ref[...], rows).astype(BF), keep_ref, away_ref)
    acc[...] += dot_columns(rows, weave(section_ref, mine_ref, other_ref))

    @pl.when(step == 0)
    def _():
        dvec_ref[2:3, :] = column_sums(rows.astype(F32))

    @pl.when(step == 2)
    def _():
        dvec_ref[3:4, :] = column_sums(rows.astype(F32))
        dn1 = acc[...]
        unit, scale = normalized(x_ref[...].astype(F32))
        dx_ref[...] = (dx1_ref[...] + norm_back(dn1, vec_ref[0:1, :], unit, scale)).astype(BF)
        dvec_ref[0:1, :] = column_sums(dn1 * unit)
        dvec_ref[1:2, :] = column_sums(dn1)


def whole(*shape):
    return pl.BlockSpec(shape, lambda *_: (0,) * len(shape))


def stepped(*shape):
    return pl.BlockSpec(shape, lambda step: (step,) + (0,) * (len(shape) - 1))


def out(shape, kind):
    return jax.ShapeDtypeStruct(shape, kind)


def params():
    return pltpu.CompilerParams(vmem_limit_bytes=VMEM_BYTES)


def cost(us):
    return pl.CostEstimate(
        flops=int(us * 4e8), bytes_accessed=int(us * 3e6), transcendentals=0
    )


def middle(rows):
    return rows // 32 * 16


def sum_pairs_kernel(*refs):
    zero_ref, one_ref, minus_ref, low_ref, high_ref, total = refs[-6:]
    pairs = refs[:-6]
    y = lax.rem(lax.axis_index("replica"), 4)
    rows, half = zero_ref.shape[1], low_ref.shape[1]
    row = 0
    for keep, got in zip(pairs[::2], pairs[1::2]):
        total[row : row + keep.shape[1], :] = add(keep[0], got[0]).astype(BF)
        row += keep.shape[1]
    if row < total.shape[0]:
        total[row:, :] = jnp.zeros((total.shape[0] - row, WIDTH), BF)

    def piece(k):
        return total[pl.ds(pl.multiple_of(lax.rem(y + k, 4) * rows, 16), rows), :]

    zero_ref[0] = piece(0)
    one_ref[0] = piece(1)
    minus_ref[0] = piece(3)
    two = piece(2)
    low_ref[0] = two[:half]
    high_ref[0] = two[half:]


def sum_pairs(pairs):
    rows = (sum(keep.shape[1] for keep, _ in pairs) + 63) // 64 * 16
    half = middle(rows)
    specs = [
        pl.BlockSpec((1, keep.shape[1], WIDTH), lambda step: (step, 0, 0))
        for keep, _ in pairs
        for _ in range(2)
    ]
    shapes = [(GROUPS, count, WIDTH) for count in (rows, rows, rows, half, rows - half)]
    return pl.pallas_call(
        sum_pairs_kernel,
        grid=(GROUPS,),
        in_specs=specs,
        out_specs=[stepped(1, *shape[1:]) for shape in shapes],
        out_shape=[out(shape, BF) for shape in shapes],
        scratch_shapes=[pltpu.VMEM((4 * rows, WIDTH), BF)],
        compiler_params=params(),
        cost_estimate=cost(5),
        name="sum_pairs",
    )(*(value for pair in pairs for value in pair))


def sum_pairs_z_kernel(*refs):
    own_ref, low_ref, high_ref = refs[-3:]
    pairs = refs[:-3]
    on_first = lax.axis_index("group") % 2 == 0
    cut = low_ref.shape[1]
    total = [add(keep[...], got[...]).astype(BF) for keep, got in zip(pairs[::2], pairs[1::2])]
    total = jnp.concatenate(total, axis=1) if len(total) > 1 else total[0]
    own_ref[0] = lax.select(on_first, total[0], total[1])
    away = lax.select(on_first, total[1], total[0])
    low_ref[0] = away[:cut]
    high_ref[0] = away[cut:]


def sum_pairs_z(pairs):
    rows = sum(keep.shape[1] for keep, _ in pairs)
    cut = middle(rows)
    specs = [
        pl.BlockSpec((2, keep.shape[1], WIDTH), lambda step: (step, 0, 0))
        for keep, _ in pairs
        for _ in range(2)
    ]
    return pl.pallas_call(
        sum_pairs_z_kernel,
        grid=(4,),
        in_specs=specs,
        out_specs=[stepped(1, rows, WIDTH), stepped(1, cut, WIDTH), stepped(1, rows - cut, WIDTH)],
        out_shape=[
            out((4, rows, WIDTH), BF),
            out((4, cut, WIDTH), BF),
            out((4, rows - cut, WIDTH), BF),
        ],
        compiler_params=params(),
        cost_estimate=cost(5),
        name="sum_pairs_z",
    )(*(value for pair in pairs for value in pair))


def sum_y_kernel(zero_ref, one_ref, minus_ref, own_ref, low_ref, high_ref):
    z = lax.axis_index("group") % 2
    cut = low_ref.shape[1]

    def total(at):
        return (add(zero_ref[at], one_ref[at]) + minus_ref[at].astype(F32)).astype(BF)

    for x in range(4):
        own_ref[x] = total(2 * x + z)
        away = total(2 * x + 1 - z)
        low_ref[x] = away[:cut]
        high_ref[x] = away[cut:]


def sum_y(zero, one, minus):
    rows = zero.shape[1]
    cut = middle(rows)
    vmem = pl.BlockSpec(memory_space=pltpu.VMEM)
    return pl.pallas_call(
        sum_y_kernel,
        in_specs=[vmem] * 3,
        out_specs=[vmem] * 3,
        out_shape=[
            out((4, rows, WIDTH), BF),
            out((4, cut, WIDTH), BF),
            out((4, rows - cut, WIDTH), BF),
        ],
        compiler_params=params(),
        cost_estimate=cost(4),
        name="sum_y",
    )(zero, one, minus)


def sum_z_kernel(own_ref, low_ref, high_ref, zero_ref, one_ref, minus_ref, two_low_ref, two_high_ref):
    x = lax.axis_index("group") // 2
    cut, half = low_ref.shape[1], two_low_ref.shape[0]

    def piece(k):
        at = lax.rem(x + k, 4)
        from_z = jnp.concatenate([low_ref[at], high_ref[at]], axis=0)
        return add(own_ref[at], from_z).astype(BF)

    zero_ref[...] = piece(0)
    one_ref[...] = piece(1)
    minus_ref[...] = piece(3)
    two = piece(2)
    two_low_ref[...] = two[:half]
    two_high_ref[...] = two[half:]


def sum_z(own, low, high):
    rows = own.shape[1]
    half = middle(rows)
    vmem = pl.BlockSpec(memory_space=pltpu.VMEM)
    return pl.pallas_call(
        sum_z_kernel,
        in_specs=[vmem] * 3,
        out_specs=[vmem] * 5,
        out_shape=[out((rows, WIDTH), BF)] * 3 + [out((half, WIDTH), BF), out((rows - half, WIDTH), BF)],
        compiler_params=params(),
        cost_estimate=cost(4),
        name="sum_z",
    )(own, low, high)


def sum_far_kernel(one_ref, minus_ref, left_ref, right_ref, one_out, minus_out):
    half = left_ref.shape[-2]
    one_out[..., :half, :] = add(one_ref[..., :half, :], left_ref[...]).astype(BF)
    one_out[..., half:, :] = one_ref[..., half:, :]
    minus_out[..., :half, :] = minus_ref[..., :half, :]
    minus_out[..., half:, :] = add(minus_ref[..., half:, :], right_ref[...]).astype(BF)


def sum_far(one, minus, from_left, from_right):
    vmem = pl.BlockSpec(memory_space=pltpu.VMEM)
    return pl.pallas_call(
        sum_far_kernel,
        in_specs=[vmem] * 4,
        out_specs=[vmem] * 2,
        out_shape=[out(one.shape, BF)] * 2,
        compiler_params=params(),
        cost_estimate=cost(2),
        name="sum_far",
    )(one, minus, from_left, from_right)


SMEM_SPEC = pl.BlockSpec(memory_space=pltpu.SMEM)
HEADS_SPEC = pl.BlockSpec((GROUPS, 1, ROWS, 128), lambda step: (0, step, 0, 0))
WIDE_SPEC = pl.BlockSpec((GROUPS, HALF, WIDTH), lambda step: (0, step, 0))
OUT_SPEC = pl.BlockSpec((GROUPS, HALF, WIDTH), lambda step: (0, 3, 0))
PROJ_SPEC = pl.BlockSpec((2, 4 * HALF, WIDTH), lambda step: (step, 1, 0))
DPROJ_SPEC = pl.BlockSpec((2, 4 * HALF, WIDTH), lambda step: (step, 0, 0))


def run_pre_forward(section, x, vec, slim):
    return pl.pallas_call(
        pre_forward,
        grid=(3,),
        in_specs=[SMEM_SPEC, whole(ROWS, WIDTH), whole(12, WIDTH), WIDE_SPEC, WIDE_SPEC],
        out_specs=[whole(ROWS, WIDTH), HEADS_SPEC],
        out_shape=[out((ROWS, WIDTH), BF), out((GROUPS, 3, ROWS, 128), BF)],
        compiler_params=params(),
        cost_estimate=cost(4),
        name="pre_forward",
    )(section, x, vec, *slim)


def run_attend_forward(length_row, qkv):
    return pl.pallas_call(
        attend_forward,
        grid=(1,),
        in_specs=[SMEM_SPEC, whole(GROUPS, 3, ROWS, 128)],
        out_specs=[whole(GROUPS, ROWS, 128), whole(SEQ, 128)],
        out_shape=[out((GROUPS, ROWS, 128), BF), out((SEQ, 128), F32)],
        compiler_params=params(),
        cost_estimate=cost(8),
        name="attend_forward",
    )(length_row, qkv)


def run_attend_backward(length_row, qkv, grad, logsum):
    return pl.pallas_call(
        attend_backward,
        grid=(1,),
        in_specs=[
            SMEM_SPEC,
            whole(GROUPS, 3, ROWS, 128),
            whole(GROUPS, ROWS, 128),
            whole(SEQ, 128),
        ],
        out_specs=whole(GROUPS, 3, ROWS, 128),
        out_shape=out((GROUPS, 3, ROWS, 128), BF),
        scratch_shapes=[pltpu.VMEM((SEQ, 128), F32), pltpu.VMEM((SEQ, 128), F32)],
        compiler_params=params(),
        cost_estimate=cost(16),
        name="attend_backward",
    )(length_row, qkv, grad, logsum)


def run_post_forward(section, mixed, x, vec, slim, wide):
    return pl.pallas_call(
        post_forward,
        grid=(4,),
        in_specs=[
            SMEM_SPEC,
            whole(GROUPS, ROWS, 128),
            whole(ROWS, WIDTH),
            whole(12, WIDTH),
            OUT_SPEC,
            OUT_SPEC,
            WIDE_SPEC,
            WIDE_SPEC,
            PROJ_SPEC,
            PROJ_SPEC,
        ],
        out_specs=[
            whole(ROWS, WIDTH),
            whole(ROWS, WIDTH),
            whole(ROWS, WIDTH),
            stepped(1, ROWS, WIDTH),
        ],
        out_shape=[
            out((ROWS, WIDTH), BF),
            out((ROWS, WIDTH), F32),
            out((ROWS, WIDTH), BF),
            out((4, ROWS, WIDTH), F32),
        ],
        scratch_shapes=[pltpu.VMEM((ROWS, WIDTH), F32)],
        compiler_params=params(),
        cost_estimate=cost(8),
        name="post_forward",
    )(section, mixed, x, vec, *slim, *wide, *wide)


def run_post_backward(section, dy, u, n2, x1, mixed, vec, slim, wide):
    return pl.pallas_call(
        post_backward,
        grid=(4,),
        in_specs=[
            SMEM_SPEC,
            whole(ROWS, WIDTH),
            stepped(1, ROWS, WIDTH),
            whole(ROWS, WIDTH),
            whole(ROWS, WIDTH),
            whole(GROUPS, ROWS, 128),
            whole(12, WIDTH),
            OUT_SPEC,
            OUT_SPEC,
            WIDE_SPEC,
            WIDE_SPEC,
            PROJ_SPEC,
            PROJ_SPEC,
        ],
        out_specs=[
            whole(ROWS, WIDTH),
            whole(GROUPS, ROWS, 128),
            whole(12, WIDTH),
            whole(GROUPS, HALF, WIDTH),
            whole(GROUPS, HALF, WIDTH),
            WIDE_SPEC,
            WIDE_SPEC,
            DPROJ_SPEC,
            DPROJ_SPEC,
        ],
        out_shape=[
            out((ROWS, WIDTH), F32),
            out((GROUPS, ROWS, 128), BF),
            out((12, WIDTH), F32),
            out((GROUPS, HALF, WIDTH), BF),
            out((GROUPS, HALF, WIDTH), BF),
            out((GROUPS, 4 * HALF, WIDTH), BF),
            out((GROUPS, 4 * HALF, WIDTH), BF),
            out((GROUPS, 4 * HALF, WIDTH), BF),
            out((GROUPS, 4 * HALF, WIDTH), BF),
        ],
        scratch_shapes=[pltpu.VMEM((ROWS, WIDTH), F32)],
        compiler_params=params(),
        cost_estimate=cost(14),
        name="post_backward",
    )(section, dy, u, n2, x1, mixed, vec, *slim, *wide, *wide)


def run_pre_backward(section, grads, n1, x, dx1, vec, slim):
    return pl.pallas_call(
        pre_backward,
        grid=(3,),
        in_specs=[
            SMEM_SPEC,
            HEADS_SPEC,
            whole(ROWS, WIDTH),
            whole(ROWS, WIDTH),
            whole(ROWS, WIDTH),
            whole(12, WIDTH),
            WIDE_SPEC,
            WIDE_SPEC,
        ],
        out_specs=[whole(ROWS, WIDTH), whole(12, WIDTH), WIDE_SPEC, WIDE_SPEC],
        out_shape=[
            out((ROWS, WIDTH), BF),
            out((12, WIDTH), F32),
            out((GROUPS, 3 * HALF, WIDTH), BF),
            out((GROUPS, 3 * HALF, WIDTH), BF),
        ],
        scratch_shapes=[pltpu.VMEM((ROWS, WIDTH), F32)],
        compiler_params=params(),
        cost_estimate=cost(0.05),
        name="pre_backward",
    )(section, grads, n1, x, dx1, vec, *slim)


def exchange(value):
    return lax.all_to_all(value, "group", 0, 0, tiled=True)


def body(
    tokens,
    cotangent,
    lengths,
    ln1_gain,
    ln1_bias,
    w_qkv,
    b_query,
    b_value,
    w_out,
    b_out,
    ln2_gain,
    ln2_bias,
    w_fc,
    b_fc,
    w_proj,
    b_proj,
):
    section = lax.axis_index("section")
    which = section.astype(jnp.int32).reshape(1)
    length_row = lax.dynamic_index_in_dim(lengths, section, 0, keepdims=False)
    tokens_row = lax.dynamic_index_in_dim(tokens, section, 0, keepdims=False)

    vectors = (ln1_gain, ln1_bias, b_query, b_value, b_out, ln2_gain, ln2_bias, b_proj)
    keep, away = run_pack_shard(which, w_qkv, w_out, w_fc, w_proj, b_fc, *vectors)
    got = swap(away)
    shard_zero, shard_one = pick(keep, got), pick(got, keep)
    front = SLIM + VEC_ROWS
    slim_zero = Gather(jnp.concatenate([shard_zero[:front], shard_one[SLIM:front]], axis=0))
    wide_zero = Gather(shard_zero[front:])
    slim_one = Gather(shard_one[:SLIM])
    wide_one = Gather(shard_one[front:])

    slim_zero.near()
    wide_zero.shard = slim_zero.after(wide_zero.shard)
    slim_zero.far()
    wide_zero.shard = slim_zero.after(wide_zero.shard)
    slim_zero.last()
    wide_zero.near()
    mine = slim_zero.whole()
    slim = mine, swap(mine)
    vecs = run_unpack_vectors(mine)

    n1, send = run_pre_forward(which, tokens_row, vecs[0], slim)
    send = wide_zero.after(send)
    slim_one.shard, send = tie(slim_one.shard, send)
    wide_zero.far()
    slim_one.near()
    heads = exchange(send)
    heads = wide_zero.after(heads)
    heads = slim_one.after(heads)
    wide_zero.last()
    slim_one.far()
    mixed, logsum = run_attend_forward(length_row, heads)
    mixed = wide_zero.after(mixed)
    mixed = slim_one.after(mixed)
    slim_one.last()
    mine = wide_zero.whole()
    wide = mine, swap(mine)
    mixed = exchange(mixed)
    mixed = slim_one.after(mixed)
    wide_one.shard, mixed = tie(wide_one.shard, mixed)
    wide_one.near()
    mine = slim_one.whole()
    slim_next = mine, swap(mine)
    result, x1, n2, u = run_post_forward(which, mixed, tokens_row, vecs[0], slim, wide)
    kept_zero = (tokens_row, n1, heads, logsum, mixed, x1, n2, u, slim, wide)

    output_zero = result
    slim = slim_next
    n1, send = run_pre_forward(which, result, vecs[1], slim)
    send = wide_one.after(send)
    wide_one.far()
    heads = exchange(send)
    heads = wide_one.after(heads)
    wide_one.last()
    mine = wide_one.whole()
    wide = mine, swap(mine)
    mixed, logsum = run_attend_forward(length_row, heads)
    mixed = exchange(mixed)
    output_one, x1, n2, u = run_post_forward(which, mixed, result, vecs[1], slim, wide)
    kept_one = (result, n1, heads, logsum, mixed, x1, n2, u, slim, wide)

    def first_part(layer, grad, kept):
        _, _, _, _, mixed, x1, n2, u, slim, wide = kept
        dx1, send, dvec, *halves = run_post_backward(
            which, grad, u, n2, x1, mixed, vecs[layer], slim, wide
        )
        pairs = [(keep, swap(away)) for keep, away in zip(halves[::2], halves[1::2])]
        return dx1, send, dvec, pairs

    def second_part(layer, dheads, dx1, kept):
        rows, n1, _, _, _, _, _, _, slim, _ = kept
        grad, dvec, keep, away = run_pre_backward(which, dheads, n1, rows, dx1, vecs[layer], slim)
        return grad, dvec, (keep, swap(away))

    far = ("from_left", "from_right")
    near = ("zero", "one", "minus")
    grad = lax.dynamic_index_in_dim(cotangent, section, 0, keepdims=False)
    dx1, send, dvec_two, pairs = first_part(1, grad, kept_one)
    bulk_one = BulkSum(pairs)
    bulk_one.y_far()
    dheads = run_attend_backward(length_row, kept_one[2], exchange(send), kept_one[3])
    dheads = exchange(dheads)
    dheads = after(bulk_one, far, dheads)
    bulk_one.y_near()
    grad_one, dvec_one, slim_pair = second_part(1, dheads, dx1, kept_one)
    dvec_last = dvec_one + dvec_two

    dx1, send, dvec_two, pairs = first_part(0, grad_one, kept_zero)
    pairs = [*pairs, slim_pair]
    grad_heads = exchange(send)
    *keeps, grad_heads = tie(*(keep for keep, _ in pairs), grad_heads)
    bulk = GroupSum([(keep, got) for keep, (_, got) in zip(keeps, pairs)])
    dheads = run_attend_backward(length_row, kept_zero[2], grad_heads, kept_zero[3])
    dheads = exchange(dheads)
    dheads = after(bulk, ("own", "low", "high"), dheads)
    dheads = after(bulk_one, near, dheads)
    bulk.far()
    bulk_one.over_z()
    grad_zero, dvec_one, (keep, got) = second_part(0, dheads, dx1, kept_zero)
    dvecs = jnp.stack([dvec_one + dvec_two, dvec_last])
    last = run_pack_last(keep, got, dvecs, swap(dvecs))
    last = after(bulk, far, last)
    last = after(bulk_one, ("own", "low", "high"), last)
    bulk.near()
    bulk_one.x_far()
    piece = last.shape[1] // 8
    arrived = lax.all_to_all(
        last.reshape(64, piece, WIDTH), ("group", "replica"), 0, 0, tiled=True
    )
    y = lax.rem(lax.axis_index("replica"), 4)
    quarter = bulk.zero.shape[0] // 4
    ring = DirectSum(bulk.total().astype(BF).reshape(4, quarter, WIDTH), y, along_y)
    bulk_one.x_near()
    after(bulk_one, near, arrived)
    arrived = after(ring, ("one", "two", "minus"), arrived)
    both, last = every_part(
        jnp.concatenate([ring.total(), bulk_one.total()], axis=0),
        jnp.sum(arrived.astype(F32), axis=0).astype(BF),
    )
    bulk, sum_one = both[:, :quarter].reshape(-1, WIDTH), both[:, quarter:].reshape(-1, WIDTH)
    split = HALF + WIDE
    sum_one = sum_one[:split]

    def own_layer(zero, one):
        mine, other = pick(zero, one), swap(pick(one, zero))
        return pick(mine, other).astype(F32), pick(other, mine).astype(F32)

    first, second = own_layer(bulk[:split], sum_one)
    first_slim, second_slim = own_layer(last[: 3 * HALF], bulk[split:])

    def block(low, high, j):
        at = slice(HALF * j, HALF * j + HALF)
        return jnp.concatenate([low[at], high[at]], axis=0)

    grad_qkv = jnp.concatenate([block(first_slim, second_slim, j) for j in range(3)], axis=1)
    grad_out = block(first, second, 0)
    grad_fc = jnp.concatenate([block(first, second, 1 + j) for j in range(4)], axis=1)
    grad_proj = jnp.concatenate([first[5 * HALF :], second[5 * HALF :]], axis=0)
    v = last[3 * HALF :].astype(F32)
    v = pick(v[:VEC_ROWS], v[VEC_ROWS:])

    def both_micro(zero, one):
        mine, other = pick(zero, one), swap(pick(one, zero))
        return jnp.stack([pick(mine, other), pick(other, mine)])[None]

    acts = both_micro(output_zero, output_one)
    in_grads = both_micro(grad_zero, grad_one)
    return (
        acts,
        in_grads,
        v[0:1, :SHARD],
        v[1:2, :SHARD],
        grad_qkv[None],
        v[2:3, :SHARD],
        v[3:4, :SHARD],
        grad_out[None],
        v[4:5, :SHARD],
        v[5:6, :SHARD],
        v[6:7, :SHARD],
        grad_fc[None],
        v[8:9, : 4 * SHARD],
        grad_proj[None],
        v[7:8, :SHARD],
    )


def solution(mesh):
    placed = (
        P("replica", "group", None),
        P("replica", "group", None),
        P("replica", None),
        P("section", "group"),
        P("section", "group"),
        P("section", "group", None),
        P("section", "group"),
        P("section", "group"),
        P("section", "group", None),
        P("section", "group"),
        P("section", "group"),
        P("section", "group"),
        P("section", "group", None),
        P("section", "group"),
        P("section", "group", None),
        P("section", "group"),
    )
    return jax.shard_map(
        body,
        mesh=mesh,
        in_specs=placed,
        out_specs=(
            P("section", "replica", "group", None),
            P("section", "replica", "group", None),
            P("section", "group"),
            P("section", "group"),
            P("section", "group", None),
            P("section", "group"),
            P("section", "group"),
            P("section", "group", None),
            P("section", "group"),
            P("section", "group"),
            P("section", "group"),
            P("section", "group", None),
            P("section", "group"),
            P("section", "group", None),
            P("section", "group"),
        ),
        check_vma=False,
    )
```
